256 devices in a mesh: narrow: 4 (over x), wide: 64 (over y, z, core).
Axes of the slice: x: 4, y: 4, z: 8, core: 2. Of those that a mesh axis runs over, the one named last changes fastest.
Arguments:
- deflation: bfloat16 [8, 3, 16, 512, 256], P(None, None, 'narrow', 'wide'), may hold values from 0.25 to 1
- residual: float32 [3, 16, 512, 256], P(None, 'narrow', 'wide'), may hold values from -1 to 2
- stiffness: float32 [16, 512, 256], P('narrow', 'wide'), may hold values from 0.25 to 2.5
- mass: float32 [16, 512, 256], P('narrow', 'wide'), may hold values from 1 to 4
- stencil: float32 [27, 3, 3], replicated, may hold values from -0.625 to 0.625
- local_inverse: bfloat16 [12, 12, 12, 320, 256], P(None, None, 'narrow', 'wide'), may hold values from -1.75 to 1.75
- inverse_factor: float32 [2048, 2048], P(('narrow', 'wide')), as said below
- margin_range: int32 [4, 64, 2, 2], P('narrow', 'wide'), may hold values from 0 to 10, as said below
- neighbor_blocks: int32 [4, 64, 9], P('narrow', 'wide'), may hold values from -1 to 255, as said below
Outputs:
- preconditioned: float32 [3, 16, 512, 256], P(None, 'narrow', 'wide')
- coarse_blocks: float32 [4, 64, 9, 8, 8], P('narrow', 'wide')
- coarse_solution: float32 [2048], replicated
The draws below stay inside these ranges and needn't reach their ends.
Inputs may be any that keep to these rules, and one draw needn't show every extreme that they name: `margin_range`: starts are 0 or 1, stops are 5 or 6 along the first dimension and 9 or 10 along the second. `neighbor_blocks`: entry (i, j, (dx + 1) * 3 + dy + 1) is the coarse block number of subdomain (i + dx, j + dy), or -1 if that lies outside the subdomain grid; the numbers of the subdomains are a permutation of 0 to 4 * 64 - 1. `inverse_factor`: zero above the diagonal.
All inputs are finite; a program needn't handle non-finite values.
Results may differ from the reference program's by a relative error of at most 0.0025.
Values may be sent and summed in bfloat16 or wider, within the bound.
No kernel may reach another device: no remote copies, remote signals or barrier semaphores. Data moves between devices by JAX's collectives and lax.ppermute only.
A program may use at most 128 MiB of HBM per device.

```python
import math
import jax
import jax.numpy as jnp
from jax import lax

CX = 4
CY = 8
CZ = 256
VECTORS = 8
BLOCKS_X = 3
BLOCKS_Y = 5
NX = 16
NY = 512
NZ = 256
COARSE = 2048
N_NARROW = 4
N_WIDE = 64


def draw_inverse_factor(key, part):
    key = jax.random.fold_in(key, 7)
    first_key, second_key = jax.random.split(key)
    scale = (3.0 * CX * CY * CZ * VECTORS * 6.0) ** (-0.5)
    diagonal = jax.random.uniform(first_key, (COARSE,), jnp.float32, 1.0, 2.0)
    lower = jax.random.normal(second_key, (COARSE, COARSE), jnp.float32) * 0.3
    lower = jnp.tril(lower * COARSE ** (-0.5), -1)
    return (scale * (jnp.diag(diagonal) + lower)).astype(jnp.float32)


def draw_margin_range(key, part):
    key = jax.random.fold_in(key, 5)
    steps = jax.random.randint(key, (N_NARROW, N_WIDE, 2, 2), 0, 2).astype(jnp.int32)
    base = jnp.array([[0, CX + 1], [0, CY + 1]], jnp.int32)
    ranges = base[None, None] + steps
    widest = jnp.array([[0, CX + 2], [0, CY + 2]], jnp.int32)
    ranges = ranges.at[0, 0].set(widest)
    return ranges.astype(jnp.int32)


def draw_neighbor_blocks(key, part):
    key = jax.random.fold_in(key, 11)
    order = jax.random.permutation(key, N_NARROW * N_WIDE).astype(jnp.int32).reshape(N_NARROW, N_WIDE)
    padded = jnp.pad(order, 1, constant_values=-1)
    pieces = [padded[1 + shift_x:1 + shift_x + N_NARROW, 1 + shift_y:1 + shift_y + N_WIDE] for shift_x in (-1, 0, 1) for shift_y in (-1, 0, 1)]
    return jnp.stack(pieces, axis=-1).astype(jnp.int32)


def levels(rng, shape, cuts, least, high):
    def one(position, shards_of):
        draws = jax.random.uniform(jax.random.fold_in(jax.random.fold_in(rng, 6), position), (shards_of,), jnp.float32, least / len(cuts), high / len(cuts))
        return jnp.repeat(jnp.exp(draws), shape[position] // shards_of).reshape((-1,) + (1,) * (len(shape) - position - 1))

    loudness = one(*cuts[0])
    for cut in cuts[1:]:
        loudness = loudness * one(*cut)
    return loudness


def bell_draw(stream_key, extent, deviation, reach, cuts=(), held_as=jnp.bfloat16):
    level = levels(stream_key, extent, cuts, -0.22, 0.18) if cuts else 1.0
    values = jax.random.normal(stream_key, extent, jnp.float32) * deviation * level
    return jnp.minimum(jnp.maximum(values, -reach), reach).astype(held_as)


def setup_inputs(seed: int = 0) -> dict:
    key_of = jax.random.split(jax.random.key(seed), 10)
    deflation = jnp.clip(0.25 + 0.75 * jax.random.uniform(key_of[0], (VECTORS, 3, NX, NY, NZ), jnp.float32) ** levels(key_of[0], (VECTORS, 3, NX, NY, NZ), ((2, 4), (3, 64)), -0.2, 0.2), 0.25, 1.0).astype(jnp.bfloat16)
    residual = jnp.clip(-1.0 + 3.0 * jax.random.uniform(key_of[1], (3, NX, NY, NZ), jnp.float32) ** levels(key_of[1], (3, NX, NY, NZ), ((1, 4), (2, 64)), -0.2, 0.2), -1.0, 2.0)
    stiffness = jnp.clip(jnp.exp(math.log(2.5) - 2.3025851 * jax.random.uniform(key_of[2], (NX, NY, NZ), jnp.float32) ** levels(key_of[2], (NX, NY, NZ), ((0, 4), (1, 64)), -0.2, 0.2)), 0.25, 2.5)
    mass = jnp.clip(jnp.exp(math.log(4.0) - 1.3862944 * jax.random.uniform(key_of[3], (NX, NY, NZ), jnp.float32) ** levels(key_of[3], (NX, NY, NZ), ((0, 4), (1, 64)), -0.2, 0.2)), 1.0, 4.0)
    stencil = bell_draw(key_of[4], (27, 3, 3), 81 ** -0.5, 0.625, (), jnp.float32)
    local_inverse = bell_draw(key_of[5], (12, 12, BLOCKS_X * N_NARROW, BLOCKS_Y * N_WIDE, NZ), 12 ** -0.5, 1.75, ((2, 4), (3, 64)))
    inverse_factor = draw_inverse_factor(jax.random.fold_in(key_of[9], 71), 0)
    margin_range = draw_margin_range(jax.random.fold_in(key_of[9], 71), 0)
    neighbor_blocks = draw_neighbor_blocks(jax.random.fold_in(key_of[9], 71), 0)
    return dict(deflation=deflation, residual=residual, stiffness=stiffness, mass=mass, stencil=stencil, local_inverse=local_inverse, inverse_factor=inverse_factor, margin_range=margin_range, neighbor_blocks=neighbor_blocks)


def side_table(shift, cells):
    where_to = jnp.arange(cells) + shift
    classes = jnp.where(where_to < 0, 0, jnp.where(where_to >= cells, 2, 1))
    return (classes[:, None] == jnp.arange(3)[None, :]).astype(jnp.float32)


def coarse_blocks_of(padded, stencil, stiffness, mass):
    vectors, components, ext_x, ext_y, depth = padded.shape
    cells_x = ext_x - 2
    cells_y = ext_y - 2
    deep = jnp.pad(padded, ((0, 0), (0, 0), (0, 0), (0, 0), (1, 1)))
    own = padded[:, :, 1:cells_x + 1, 1:cells_y + 1, :]
    blocks = jnp.zeros((3, 3, vectors, vectors), jnp.float32)
    for shift_x in (-1, 0, 1):
        for shift_y in (-1, 0, 1):
            image = jnp.zeros(own.shape, jnp.float32)
            for shift_z in (-1, 0, 1):
                piece = deep[:, :, 1 + shift_x:1 + shift_x + cells_x, 1 + shift_y:1 + shift_y + cells_y, 1 + shift_z:1 + shift_z + depth]
                offset = ((shift_x + 1) * 3 + shift_y + 1) * 3 + shift_z + 1
                image = image + jnp.einsum("ij,ajxyz->aixyz", stencil[offset], piece, precision=lax.Precision.HIGHEST)
            image = stiffness * image
            if shift_x == 0 and shift_y == 0:
                image = image + mass * own
            products = jnp.einsum("acxyz,bcxyz->abxy", own, image, precision=lax.Precision.HIGHEST)
            blocks = blocks + jnp.einsum("abxy,xs,yt->stab", products, side_table(shift_x, cells_x), side_table(shift_y, cells_y), precision=lax.Precision.HIGHEST)
    return blocks.reshape(9, vectors, vectors)


def margin_mask(extended, ranges):
    along_x = jnp.arange(extended.shape[1])
    along_y = jnp.arange(extended.shape[2])
    keep_x = (along_x >= ranges[0, 0]) & (along_x < ranges[0, 1])
    keep_y = (along_y >= ranges[1, 0]) & (along_y < ranges[1, 1])
    keep = keep_x[:, None] & keep_y[None, :]
    return jnp.where(keep[None, :, :, None], extended, jnp.zeros_like(extended))


def local_solve(inverse, extended):
    components, ext_x, ext_y, depth = extended.shape
    half_x = ext_x // 2
    half_y = ext_y // 2
    grouped = extended.reshape(components, half_x, 2, half_y, 2, depth).transpose(0, 2, 4, 1, 3, 5).reshape(components * 4, half_x, half_y, depth)
    solved = jnp.einsum("ijxyz,jxyz->ixyz", inverse.astype(jnp.float32), grouped.astype(jnp.float32), precision=lax.Precision.HIGHEST)
    solved = solved.reshape(components, 2, 2, half_x, half_y, depth).transpose(0, 3, 1, 4, 2, 5).reshape(components, ext_x, ext_y, depth)
    return solved[:, 1:ext_x - 1, 1:ext_y - 1, :]


def reference(deflation, residual, stiffness, mass, stencil, local_inverse, inverse_factor, margin_range, neighbor_blocks):
    vectors = deflation.shape[0]
    rounded = residual.astype(jnp.bfloat16)
    padded_all = jnp.pad(deflation, ((0, 0), (0, 0), (1, 1), (1, 1), (0, 0)))
    residual_all = jnp.pad(rounded, ((0, 0), (1, 1), (1, 1), (0, 0)))
    zero = jnp.int32(0)

    def per_device(index):
        row = (index // N_WIDE).astype(jnp.int32)
        column = (index % N_WIDE).astype(jnp.int32)
        start_x = (row * CX).astype(jnp.int32)
        start_y = (column * CY).astype(jnp.int32)
        padded = lax.dynamic_slice(padded_all, (zero, zero, start_x, start_y, zero), (vectors, 3, CX + 2, CY + 2, CZ)).astype(jnp.float32)
        stiff_here = lax.dynamic_slice(stiffness, (start_x, start_y, zero), (CX, CY, CZ))
        mass_here = lax.dynamic_slice(mass, (start_x, start_y, zero), (CX, CY, CZ))
        blocks = coarse_blocks_of(padded, stencil, stiff_here, mass_here)
        own = padded[:, :, 1:CX + 1, 1:CY + 1, :]
        own_residual = lax.dynamic_slice(rounded, (zero, start_x, start_y, zero), (3, CX, CY, CZ)).astype(jnp.float32)
        rhs = jnp.einsum("acxyz,cxyz->a", own, own_residual, precision=lax.Precision.HIGHEST)
        extended = lax.dynamic_slice(residual_all, (zero, start_x, start_y, zero), (3, CX + 2, CY + 2, CZ))
        extended = margin_mask(extended, margin_range[row, column])
        inverse = lax.dynamic_slice(local_inverse, (zero, zero, (row * BLOCKS_X).astype(jnp.int32), (column * BLOCKS_Y).astype(jnp.int32), zero), (12, 12, BLOCKS_X, BLOCKS_Y, CZ))
        local = local_solve(inverse, extended)
        return blocks, rhs, local

    count = N_NARROW * N_WIDE
    blocks, rhs, local = lax.map(per_device, jnp.arange(count, dtype=jnp.int32))
    listing = neighbor_blocks.reshape(count, 9)
    own_ids = listing[:, 4]
    coarse_rhs = jnp.zeros((count, vectors), jnp.float32).at[own_ids].set(rhs).reshape(-1)

    def solve(vector):
        inner = jnp.dot(inverse_factor, vector, precision=lax.Precision.HIGHEST)
        return jnp.dot(inverse_factor.T, inner, precision=lax.Precision.HIGHEST)

    first = solve(coarse_rhs)
    table = first.reshape(count, vectors)
    valid = listing >= 0
    near = jnp.where(valid[:, :, None], table[jnp.maximum(listing, 0)], jnp.zeros((count, 9, vectors), jnp.float32))
    image = jnp.einsum("dnab,dnb->da", blocks, near, precision=lax.Precision.HIGHEST)
    coarse_image = jnp.zeros((count, vectors), jnp.float32).at[own_ids].set(image).reshape(-1)
    coarse_solution = first + solve(coarse_rhs - coarse_image)
    weights = coarse_solution.reshape(count, vectors)[own_ids]

    def finish(index):
        row = (index // N_WIDE).astype(jnp.int32)
        column = (index % N_WIDE).astype(jnp.int32)
        own = lax.dynamic_slice(deflation, (zero, zero, (row * CX).astype(jnp.int32), (column * CY).astype(jnp.int32), zero), (vectors, 3, CX, CY, CZ)).astype(jnp.float32)
        return local[index] + jnp.einsum("a,acxyz->cxyz", weights[index], own, precision=lax.Precision.HIGHEST)

    result = lax.map(finish, jnp.arange(count, dtype=jnp.int32))
    preconditioned = result.reshape(N_NARROW, N_WIDE, 3, CX, CY, CZ).transpose(2, 0, 3, 1, 4, 5).reshape(3, N_NARROW * CX, N_WIDE * CY, CZ)
    coarse_blocks = blocks.reshape(N_NARROW, N_WIDE, 9, vectors, vectors)
    return preconditioned, coarse_blocks, coarse_solution
```

```python
import functools

import jax
import jax.numpy as jnp
from jax import lax
from jax.experimental import pallas as pl
from jax.experimental.pallas import tpu as pltpu
from jax.sharding import PartitionSpec as P

F32 = jnp.float32
AXES = ("narrow", "wide")
SLOT = 80
VMEM = pl.BlockSpec(memory_space=pltpu.VMEM)
SMEM = pl.BlockSpec(memory_space=pltpu.SMEM)


def shifted(value, offset, axis):
    if offset == 0:
        return value
    size = value.shape[axis]
    rolled = pltpu.roll(value, (-offset) % size, axis)
    at = lax.broadcasted_iota(jnp.int32, value.shape, axis)
    keep = at < size - offset if offset > 0 else at >= -offset
    return jnp.where(keep, rolled, 0.0)


def rows_sum(value):
    return jnp.sum(value[:, :128] + value[:, 128:], axis=0, keepdims=True)


def entry(s_ref, ox, oy, oz, i, j):
    return s_ref[((((ox + 1) * 3 + oy + 1) * 3 + oz + 1) * 3 + i) * 3 + j]


def centre_kernel(s_ref, z_ref, r_ref, stiff_ref, mass_ref, out_ref, rhs_ref, zf_ref):
    vectors, _, cells_x = z_ref.shape[:3]

    def convert(a, carry):
        for i in range(3):
            for x in range(cells_x):
                zf_ref[a, i, x] = z_ref[a, i, x].astype(F32)
        return carry

    lax.fori_loop(0, vectors, convert, 0)
    for a in range(vectors):
        total = None
        for i in range(3):
            for x in range(cells_x):
                term = zf_ref[a, i, x] * r_ref[i, x].astype(F32)
                total = term if total is None else total + term
        rhs_ref[a : a + 1, :] = rows_sum(total)

    def one(b, carry):
        field = [[zf_ref[b, j, x] for x in range(cells_x)] for j in range(3)]
        weighted = []
        for i in range(3):
            image = [None] * cells_x
            for oz in (-1, 0, 1):
                level = [None] * cells_x
                for oy in (-1, 0, 1):
                    for x in range(cells_x):
                        acc = None
                        for ox in (-1, 0, 1):
                            if 0 <= x + ox < cells_x:
                                for j in range(3):
                                    term = entry(s_ref, ox, oy, oz, i, j) * field[j][x + ox]
                                    acc = term if acc is None else acc + term
                        acc = shifted(acc, oy, 0)
                        level[x] = acc if level[x] is None else level[x] + acc
                for x in range(cells_x):
                    moved = shifted(level[x], oz, 1)
                    image[x] = moved if image[x] is None else image[x] + moved
            weighted.append([stiff_ref[x] * image[x] + mass_ref[x] * field[i][x] for x in range(cells_x)])
        for a in range(vectors):
            total = None
            for i in range(3):
                for x in range(cells_x):
                    term = zf_ref[a, i, x] * weighted[i][x]
                    total = term if total is None else total + term
            out_ref[b, a : a + 1, :] = rows_sum(total)
        return carry

    lax.fori_loop(0, vectors, one, 0)


def edge_kernel(
    s_ref, ids_ref, z_ref, stiff_ref, xlo_ref, xhi_ref, ylo_ref, yhi_ref, centre_ref, rhs_ref,
    blocks_ref, pay_ref, r_ref, zx_ref, zy_ref, sy_ref,
):
    vectors, _, cells_x, cells_y, depth = z_ref.shape
    own_x = (0, cells_x - 1)
    own_y = (0, cells_y - 1)
    blank = jnp.zeros((8 - cells_x, depth), F32)

    def columns(rows):
        return jnp.concatenate(rows + [blank], axis=0)

    def prepare(a, carry):
        for i in range(3):
            cells = [z_ref[a, i, x].astype(F32) for x in range(cells_x)]
            for face in range(2):
                zx_ref[face, a, i] = cells[own_x[face]]
                y = own_y[face]
                zy_ref[face, a, i] = columns([cell[y : y + 1, :] for cell in cells])
        return carry

    lax.fori_loop(0, vectors, prepare, 0)
    for face in range(2):
        y = own_y[face]
        sy_ref[face] = columns([stiff_ref[x, y : y + 1, :] for x in range(cells_x)])

    row = lax.broadcasted_iota(jnp.int32, (8, depth), 0)

    def one(b, carry):
        for face, halo_ref in ((0, xlo_ref), (1, xhi_ref)):
            ox = 2 * face - 1
            field = [halo_ref[b * 3 + j].astype(F32) for j in range(3)]
            stiff = stiff_ref[own_x[face]]
            weighted = []
            for i in range(3):
                image = None
                for oz in (-1, 0, 1):
                    level = None
                    for oy in (-1, 0, 1):
                        acc = sum(entry(s_ref, ox, oy, oz, i, j) * field[j] for j in range(3))
                        acc = shifted(acc, oy, 0)
                        level = acc if level is None else level + acc
                    moved = shifted(level, oz, 1)
                    image = moved if image is None else image + moved
                weighted.append(stiff * image)
            number = 1 if face == 0 else 7
            for a in range(vectors):
                total = sum(zx_ref[face, a, i] * weighted[i] for i in range(3))
                r_ref[number * vectors + b, a : a + 1, :] = rows_sum(total)
        for face, halo_ref in ((0, ylo_ref), (1, yhi_ref)):
            oy = 2 * face - 1
            pad = jnp.zeros((8 - halo_ref.shape[1], depth), F32)
            field = [jnp.concatenate([halo_ref[b * 3 + j].astype(F32), pad], axis=0) for j in range(3)]
            stiff = sy_ref[face]
            inner, outer = [], []
            for i in range(3):
                mid, rim = None, None
                for ox in (-1, 0, 1):
                    line = None
                    for oz in (-1, 0, 1):
                        acc = sum(entry(s_ref, ox, oy, oz, i, j) * field[j] for j in range(3))
                        acc = shifted(acc, oz, 1)
                        line = acc if line is None else line + acc
                    moved = pltpu.roll(line, (-(1 + ox)) % 8, 0) if ox != -1 else line
                    low, high = max(0, -ox), min(cells_x, cells_x - ox)
                    part = jnp.where((row >= low) & (row < high), moved, 0.0)
                    mid = part if mid is None else mid + part
                    if ox != 0:
                        edge = jnp.where(row == (0 if ox == -1 else cells_x - 1), moved, 0.0)
                        rim = edge if rim is None else rim + edge
                inner.append(stiff * mid)
                outer.append(stiff * rim)
            for a in range(vectors):
                own = [zy_ref[face, a, i] for i in range(3)]
                total = sum(own[i] * inner[i] for i in range(3))
                r_ref[(3 + 2 * face) * vectors + b, a : a + 1, :] = rows_sum(total)
                total = sum(own[i] * outer[i] for i in range(3))
                half = total[:, :128] + total[:, 128:]
                r_ref[(0 + 2 * face) * vectors + b, a : a + 1, :] = half[0:1, :]
                r_ref[(6 + 2 * face) * vectors + b, a : a + 1, :] = half[cells_x - 1 : cells_x, :]
        return carry

    lax.fori_loop(0, vectors, one, 0)
    lane = lax.broadcasted_iota(jnp.int32, (8, 128), 1)
    table = jnp.zeros((8, 128), F32)
    for k in range(9 * vectors):
        piece = centre_ref[k % vectors] if k // vectors == 4 else r_ref[k]
        table = jnp.where(lane == k, jnp.sum(piece, axis=1, keepdims=True), table)
    blocks_ref[...] = table
    table = jnp.where(lane == 72, jnp.sum(rhs_ref[...], axis=1, keepdims=True), table)
    table = jnp.where(lane == 73, ids_ref[4].astype(F32), table)
    width = pay_ref.shape[1]
    wide = jnp.concatenate([table, jnp.zeros((8, width - 128), F32)], axis=1)
    line = jnp.zeros((1, width), F32)
    for a in range(vectors):
        piece = wide[a : a + 1, :]
        line = line + (pltpu.roll(piece, a * SLOT, 1) if a else piece)
    pay_ref[...] = jnp.broadcast_to(line, pay_ref.shape)


def local_kernel(range_ref, inverse_ref, r_ref, xlo_ref, xhi_ref, ylo_ref, yhi_ref, out_ref, ext_ref, sol_ref):
    cells_x, cells_y = r_ref.shape[1:3]
    ext_x, ext_y = cells_x + 2, cells_y + 2
    half_x, half_y = ext_x // 2, ext_y // 2
    first = xlo_ref.shape[0] - 3
    halves = ((0, slice(0, 128)), (1, slice(128, 256)))
    for c in range(3):
        for e in range(ext_x):
            if e == 0:
                middle = xlo_ref[first + c]
            elif e == ext_x - 1:
                middle = xhi_ref[first + c]
            else:
                middle = r_ref[c, e - 1]
            middle = middle.astype(F32)
            low = ylo_ref[first + c].astype(F32)[e : e + 1, :]
            high = yhi_ref[first + c].astype(F32)[e : e + 1, :]
            for h, lanes in halves:
                ext_ref[c, e, h, 1 : cells_y + 1, :] = middle[:, lanes]
                ext_ref[c, e, h, 0:1, :] = low[:, lanes]
                ext_ref[c, e, h, cells_y + 1 : ext_y, :] = high[:, lanes]
    at = lax.broadcasted_iota(jnp.int32, (half_y, r_ref.shape[3]), 0)
    for u in range(half_x):
        fields = []
        for m in range(12):
            c, s, t = m // 4, m // 2 % 2, m % 2
            e, f = 2 * u + s, 2 * at + t
            keep = (f >= range_ref[2]) & (f < range_ref[3]) & (e >= range_ref[0]) & (e < range_ref[1])
            value = jnp.concatenate([ext_ref[c, e, h, pl.ds(t, half_y, stride=2), :] for h, _ in halves], axis=1)
            fields.append(jnp.where(keep, value, 0.0))
        for i in range(12):
            acc = None
            for m in range(12):
                term = inverse_ref[i, m, u].astype(F32) * fields[m]
                acc = term if acc is None else acc + term
            c, s, t = i // 4, i // 2 % 2, i % 2
            for h, lanes in halves:
                sol_ref[c, 2 * u + s, h, pl.ds(t, half_y, stride=2), :] = acc[:, lanes]
    for c in range(3):
        for x in range(cells_x):
            for h, lanes in halves:
                out_ref[c, x, :, lanes] = sol_ref[c, x + 1, h, 1 : cells_y + 1, :]


def dotted(left, right, dims):
    return lax.dot_general(
        left, right, (dims, ((), ())), precision=lax.Precision.HIGHEST, preferred_element_type=F32
    )


def slots_of(packed_ref):
    count = packed_ref.shape[1]
    ids = packed_ref[73:74, :].astype(jnp.int32)
    return (lax.broadcasted_iota(jnp.int32, (count, count), 0) == ids).astype(F32)


def share_of(vector, pieces):
    line = jnp.concatenate([vector[b : b + 1, :] for b in range(8)], axis=1)
    line = jnp.broadcast_to(line, (8, line.shape[1]))
    acc = jnp.zeros(line.shape, F32)
    for piece in pieces:
        count = piece.shape[0] // 8
        group = 4 if count % 4 == 0 else 1

        def step(t, acc, piece=piece, group=group):
            tiles, inner = [], []
            for q in range(group):
                tile = piece[pl.ds(pl.multiple_of((t * group + q) * 8, 8), 8), :]
                tiles.append(tile)
                inner.append(jnp.sum(tile * line, axis=1, keepdims=True))
            for tile, value in zip(tiles, inner):
                acc = acc + tile * value
            return acc

        acc = lax.fori_loop(0, count // group, step, acc)
    total = jnp.sum(acc, axis=0, keepdims=True)
    blocks = vector.shape[1]
    return jnp.concatenate([total[:, b * blocks : (b + 1) * blocks] for b in range(8)], axis=0)


def first_kernel(got_ref, *refs):
    pieces, (packed_ref, rhs_ref, share_ref) = refs[:-3], refs[-3:]
    packed_ref[...] = got_ref[...].T
    own = jnp.concatenate([packed_ref[a * SLOT + 72 : a * SLOT + 73, :] for a in range(8)], axis=0)
    rhs = dotted(own, slots_of(packed_ref), ((1,), (1,)))
    rhs_ref[...] = rhs
    share_ref[...] = share_of(rhs, pieces)


def second_kernel(n_wide, packed_ref, rhs_ref, part_ref, got1_ref, got2_ref, got3_ref, *refs):
    pieces, (first_ref, share_ref) = refs[:-2], refs[-2:]
    first = (part_ref[...] + got1_ref[...]) + (got2_ref[...] + got3_ref[...])
    first_ref[...] = first
    slots = slots_of(packed_ref)
    there = dotted(first, slots, ((1,), (0,)))
    count = there.shape[1]
    n_narrow = count // n_wide
    at = lax.broadcasted_iota(jnp.int32, there.shape, 1)
    row, column = at // n_wide, at % n_wide
    near = []
    for dx in (-1, 0, 1):
        for dy in (-1, 0, 1):
            move = (-(dx * n_wide + dy)) % count
            value = pltpu.roll(there, move, 1) if move else there
            keep = (row + dx >= 0) & (row + dx < n_narrow) & (column + dy >= 0) & (column + dy < n_wide)
            near.append(jnp.where(keep, value, 0.0))
    near.append(jnp.zeros_like(there))
    near = jnp.concatenate(near, axis=0)
    image = jnp.concatenate(
        [jnp.sum(packed_ref[a * SLOT : (a + 1) * SLOT, :] * near, axis=0, keepdims=True) for a in range(8)], axis=0
    )
    vector = rhs_ref[...] - dotted(image, slots, ((1,), (1,)))
    share_ref[...] = share_of(vector, pieces)


def last_kernel(ids_ref, z_ref, local_ref, first_ref, part_ref, got1_ref, got2_ref, got3_ref, out_ref, sol_ref):
    solution = first_ref[...] + ((part_ref[...] + got1_ref[...]) + (got2_ref[...] + got3_ref[...]))
    sol_ref[...] = solution
    at = lax.broadcasted_iota(jnp.int32, solution.shape, 1)
    weights = jnp.sum(jnp.where(at == ids_ref[4], solution, 0.0), axis=1, keepdims=True)
    for x in range(z_ref.shape[2]):
        for i in range(3):
            acc = local_ref[i, x]
            for a in range(8):
                acc = acc + weights[a : a + 1, :] * z_ref[a, i, x].astype(F32)
            out_ref[i, x] = acc


def call(kernel, out_shape, in_specs, scratch=(), flops=0, moved=0, name=None):
    return pl.pallas_call(
        kernel,
        out_shape=[jax.ShapeDtypeStruct(shape, F32) for shape in out_shape],
        in_specs=in_specs,
        out_specs=[VMEM] * len(out_shape),
        scratch_shapes=list(scratch),
        compiler_params=pltpu.CompilerParams(vmem_limit_bytes=40 * 2**20),
        cost_estimate=pl.CostEstimate(flops=flops, bytes_accessed=moved, transcendentals=0),
        name=name,
    )


def body(
    deflation,
    residual,
    stiffness,
    mass,
    stencil,
    local_inverse,
    inverse_factor,
    margin_range,
    neighbor_blocks,
):
    vectors, _, cells_x, cells_y, depth = deflation.shape
    n_narrow, n_wide = lax.axis_size("narrow"), lax.axis_size("wide")
    count = n_narrow * n_wide
    size_z, size_c = 8, 2
    size_y = n_wide // (size_z * size_c)

    def wide_perm(step_y, step_z, step_c):
        pairs = []
        for y in range(size_y):
            for z in range(size_z):
                for c in range(size_c):
                    to = ((y + step_y) % size_y * size_z + (z + step_z) % size_z) * size_c + (c + step_c) % size_c
                    pairs.append(((y * size_z + z) * size_c + c, to))
        return pairs

    rounded = residual.astype(jnp.bfloat16)
    flat_stencil = stencil.reshape(-1)
    ids = neighbor_blocks.reshape(-1)
    ranges = margin_range.reshape(-1)

    def ends(axis):
        size = lax.axis_size(axis)
        up = [(k, k + 1) for k in range(size - 1)]
        return up, [(b, a) for a, b in up]

    up, down = ends("narrow")
    fields = jnp.concatenate([deflation.reshape(3 * vectors, cells_x, cells_y, depth), rounded], axis=0)
    xlo = lax.ppermute(fields[:, cells_x - 1], "narrow", up)
    xhi = lax.ppermute(fields[:, 0], "narrow", down)
    up, down = ends("wide")

    def side(y):
        return jnp.concatenate([xlo[:, y : y + 1], fields[:, :, y], xhi[:, y : y + 1]], axis=1)

    ylo = lax.ppermute(side(cells_y - 1), "wide", up)
    yhi = lax.ppermute(side(0), "wide", down)

    rows = inverse_factor.shape[0]
    own = inverse_factor.reshape(rows, count, vectors).transpose(0, 2, 1).reshape(rows, count * vectors)
    left = lax.ppermute(own, "wide", wide_perm(0, 1, 0))
    right = lax.ppermute(own, "wide", wide_perm(0, -1, 0))
    three = jnp.concatenate([own, left, right], axis=0)
    far_left = lax.ppermute(three, "wide", wide_perm(0, 3, 0))
    far_right = lax.ppermute(three[: 2 * rows], "wide", wide_perm(0, -3, 0))
    line = jnp.concatenate([three, far_left, far_right], axis=0)
    pieces = [line] + [lax.ppermute(line, "wide", wide_perm(step, 0, 0)) for step in range(1, size_y)]

    centre, rhs_rows = call(
        centre_kernel,
        [(vectors, vectors, 128), (vectors, 128)],
        [SMEM] + [VMEM] * 4,
        [pltpu.VMEM((vectors, 3, cells_x, cells_y, depth), F32)],
        flops=40_000_000,
        moved=1_000_000,
        name="centre",
    )(flat_stencil, deflation, rounded, stiffness, mass)
    table, payload = call(
        edge_kernel,
        [(8, 128), (count, SLOT * vectors)],
        [SMEM, SMEM] + [VMEM] * 8,
        [
            pltpu.VMEM((9 * vectors, 8, 128), F32),
            pltpu.VMEM((2, vectors, 3, 8, depth), F32),
            pltpu.VMEM((2, vectors, 3, 8, depth), F32),
            pltpu.VMEM((2, 8, depth), F32),
        ],
        flops=10_000_000,
        moved=2_000_000,
        name="edges",
    )(flat_stencil, ids, deflation, stiffness, xlo, xhi, ylo, yhi, centre, rhs_rows)
    got = lax.all_to_all(payload, AXES, 0, 0, tiled=True)
    (local,) = call(
        local_kernel,
        [(3, cells_x, cells_y, depth)],
        [SMEM] + [VMEM] * 6,
        [pltpu.VMEM((3, cells_x + 2, 2, 16, depth // 2), F32)] * 2,
        flops=2_000_000,
        moved=3_000_000,
        name="local",
    )(ranges, local_inverse, rounded, xlo, xhi, ylo, yhi)

    def spread(share):
        part = share + lax.ppermute(share, "wide", wide_perm(0, 0, 1))
        moves = [
            lax.ppermute(part, "narrow", [(k, (k + step) % n_narrow) for k in range(n_narrow)])
            for step in range(1, n_narrow)
        ]
        return [part] + moves

    packed, rhs, share = call(
        first_kernel,
        [(SLOT * vectors, count), (vectors, count), (vectors, count)],
        [VMEM] * (1 + len(pieces)),
        flops=4_000_000,
        moved=3_000_000,
        name="first",
    )(got, *pieces)
    first, share = call(
        functools.partial(second_kernel, n_wide),
        [(vectors, count), (vectors, count)],
        [VMEM] * (6 + len(pieces)),
        flops=4_000_000,
        moved=3_000_000,
        name="second",
    )(packed, rhs, *spread(share), *pieces)
    preconditioned, solved = call(
        last_kernel,
        [(3, cells_x, cells_y, depth), (vectors, count)],
        [SMEM] + [VMEM] * 7,
        flops=1_000_000,
        moved=1_000_000,
        name="last",
    )(ids, deflation, local, first, *spread(share))
    coarse_solution = solved.T.reshape(-1)
    blocks = table[:, : 9 * vectors].reshape(vectors, 9, vectors).transpose(1, 0, 2)
    return preconditioned, blocks.reshape(1, 1, 9, vectors, vectors), coarse_solution


def solution(mesh):
    placed = (
        P(None, None, "narrow", "wide", None),
        P(None, "narrow", "wide", None),
        P("narrow", "wide", None),
        P("narrow", "wide", None),
        P(),
        P(None, None, "narrow", "wide", None),
        P(("narrow", "wide"), None),
        P("narrow", "wide", None, None),
        P("narrow", "wide", None),
    )
    return jax.shard_map(
        body,
        mesh=mesh,
        in_specs=placed,
        out_specs=(P(None, "narrow", "wide", None), P("narrow", "wide", None, None, None), P()),
        check_vma=False,
    )
```

```python
import functools

import jax
import jax.numpy as jnp
from jax import lax
from jax.experimental import pallas as pl
from jax.experimental.pallas import tpu as pltpu
from jax.sharding import PartitionSpec as P

F32 = jnp.float32
WIDE = ("y", "z", "core")
SLOT = 80
VMEM = pl.BlockSpec(memory_space=pltpu.VMEM)
SMEM = pl.BlockSpec(memory_space=pltpu.SMEM)


def shifted(value, offset, axis):
    if offset == 0:
        return value
    size = value.shape[axis]
    rolled = pltpu.roll(value, (-offset) % size, axis)
    at = lax.broadcasted_iota(jnp.int32, value.shape, axis)
    keep = at < size - offset if offset > 0 else at >= -offset
    return jnp.where(keep, rolled, 0.0)


def rows_sum(value):
    return jnp.sum(value[:, :128] + value[:, 128:], axis=0, keepdims=True)


def entry(s_ref, ox, oy, oz, i, j):
    return s_ref[i, j, ((ox + 1) * 3 + oy + 1) * 3 + oz + 1]


def faces(total):
    return jnp.sum(total, axis=1, keepdims=True)


def centre_rows(b, s_ref, zf_ref, stiff_ref, mass_ref, rows_ref, place):
    vectors, _, cells_x = zf_ref.shape[:3]
    field = [[zf_ref[b, j, x] for x in range(cells_x)] for j in range(3)]
    weighted = []
    for i in range(3):
        image = [None] * cells_x
        for oz in (-1, 0, 1):
            level = [None] * cells_x
            for oy in (-1, 0, 1):
                for x in range(cells_x):
                    acc = None
                    for ox in (-1, 0, 1):
                        if 0 <= x + ox < cells_x:
                            for j in range(3):
                                term = entry(s_ref, ox, oy, oz, i, j) * field[j][x + ox]
                                acc = term if acc is None else acc + term
                    acc = shifted(acc, oy, 0)
                    level[x] = acc if level[x] is None else level[x] + acc
            for x in range(cells_x):
                moved = shifted(level[x], oz, 1)
                image[x] = moved if image[x] is None else image[x] + moved
        weighted.append([stiff_ref[x] * image[x] + mass_ref[x] * field[i][x] for x in range(cells_x)])
    for a in range(vectors):
        total = None
        for i in range(3):
            for x in range(cells_x):
                term = zf_ref[a, i, x] * weighted[i][x]
                total = term if total is None else total + term
        rows_ref[place, a : a + 1, :] = rows_sum(total)


def before_kernel(
    done, s_ref, ids_ref, z_ref, r_ref, stiff_ref, mass_ref, zf_ref, zy_ref, sy_ref, table_ref, rows_ref
):
    vectors, _, cells_x, cells_y, depth = z_ref.shape
    own_y = (0, cells_y - 1)
    blank = jnp.zeros((8 - cells_x, depth), F32)

    def columns(rows):
        return jnp.concatenate(rows + [blank], axis=0)

    def convert(a, carry):
        for i in range(3):
            cells = [z_ref[a, i, x].astype(F32) for x in range(cells_x)]
            for x in range(cells_x):
                zf_ref[a, i, x] = cells[x]
            for face, y in enumerate(own_y):
                zy_ref[face, a, i] = columns([cell[y : y + 1, :] for cell in cells])
        return carry

    lax.fori_loop(0, vectors, convert, 0)
    for face, y in enumerate(own_y):
        sy_ref[face] = columns([stiff_ref[x, y : y + 1, :] for x in range(cells_x)])
    for a in range(vectors):
        total = None
        for i in range(3):
            for x in range(cells_x):
                term = zf_ref[a, i, x] * r_ref[i, x].astype(F32)
                total = term if total is None else total + term
        rows_ref[done, a : a + 1, :] = rows_sum(total)

    def one(b, carry):
        centre_rows(b, s_ref, zf_ref, stiff_ref, mass_ref, rows_ref, b)
        return carry

    lax.fori_loop(0, done, one, 0)
    lane = lax.broadcasted_iota(jnp.int32, (8, 128), 1)
    table = jnp.where(lane == 9 * vectors + 1, ids_ref[4].astype(F32), 0.0)
    table = jnp.where(lane == 9 * vectors, faces(rows_ref[done]), table)
    for b in range(done):
        table = jnp.where(lane == 4 * vectors + b, faces(rows_ref[b]), table)
    table_ref[...] = table


def inner_kernel(done, s_ref, zf_ref, stiff_ref, mass_ref, xlo_ref, xhi_ref, before_ref, table_ref, rows_ref):
    vectors, _, cells_x = zf_ref.shape[:3]
    own_x = (0, cells_x - 1)

    def one(b, carry):
        centre_rows(b, s_ref, zf_ref, stiff_ref, mass_ref, rows_ref, vectors + b)
        return carry

    lax.fori_loop(done, vectors, one, 0)

    def other(b, carry):
        for face, halo_ref in ((0, xlo_ref), (1, xhi_ref)):
            ox = 2 * face - 1
            field = [halo_ref[b * 3 + j].astype(F32) for j in range(3)]
            stiff = stiff_ref[own_x[face]]
            weighted = []
            for i in range(3):
                image = None
                for oz in (-1, 0, 1):
                    level = None
                    for oy in (-1, 0, 1):
                        acc = sum(entry(s_ref, ox, oy, oz, i, j) * field[j] for j in range(3))
                        acc = shifted(acc, oy, 0)
                        level = acc if level is None else level + acc
                    moved = shifted(level, oz, 1)
                    image = moved if image is None else image + moved
                weighted.append(stiff * image)
            for a in range(vectors):
                total = sum(zf_ref[a, i, own_x[face]] * weighted[i] for i in range(3))
                rows_ref[2 * face * vectors + b, a : a + 1, :] = rows_sum(total)
        return carry

    lax.fori_loop(0, vectors, other, 0)
    lane = lax.broadcasted_iota(jnp.int32, (8, 128), 1)
    table = before_ref[...]
    for place, number in enumerate((1, 4, 7)):
        for b in range(done if number == 4 else 0, vectors):
            table = jnp.where(lane == number * vectors + b, faces(rows_ref[place * vectors + b]), table)
    table_ref[...] = table


def outer_kernel(s_ref, table_ref, zy_ref, sy_ref, ylo_ref, yhi_ref, blocks_ref, pay_ref, rows_ref):
    vectors, depth = zy_ref.shape[1], zy_ref.shape[4]
    cells_x = ylo_ref.shape[1] - 2
    row = lax.broadcasted_iota(jnp.int32, (8, depth), 0)

    def one(b, carry):
        for face, halo_ref in ((0, ylo_ref), (1, yhi_ref)):
            oy = 2 * face - 1
            pad = jnp.zeros((8 - halo_ref.shape[1], depth), F32)
            field = [jnp.concatenate([halo_ref[b * 3 + j].astype(F32), pad], axis=0) for j in range(3)]
            stiff = sy_ref[face]
            inner, outer = [], []
            for i in range(3):
                mid, rim = None, None
                for ox in (-1, 0, 1):
                    line = None
                    for oz in (-1, 0, 1):
                        acc = sum(entry(s_ref, ox, oy, oz, i, j) * field[j] for j in range(3))
                        acc = shifted(acc, oz, 1)
                        line = acc if line is None else line + acc
                    moved = pltpu.roll(line, (-(1 + ox)) % 8, 0) if ox != -1 else line
                    low, high = max(0, -ox), min(cells_x, cells_x - ox)
                    part = jnp.where((row >= low) & (row < high), moved, 0.0)
                    mid = part if mid is None else mid + part
                    if ox != 0:
                        edge = jnp.where(row == (0 if ox == -1 else cells_x - 1), moved, 0.0)
                        rim = edge if rim is None else rim + edge
                inner.append(stiff * mid)
                outer.append(stiff * rim)
            for a in range(vectors):
                own = [zy_ref[face, a, i] for i in range(3)]
                total = sum(own[i] * inner[i] for i in range(3))
                rows_ref[(3 * face + 1) * vectors + b, a : a + 1, :] = rows_sum(total)
                total = sum(own[i] * outer[i] for i in range(3))
                half = total[:, :128] + total[:, 128:]
                rows_ref[3 * face * vectors + b, a : a + 1, :] = half[0:1, :]
                rows_ref[(3 * face + 2) * vectors + b, a : a + 1, :] = half[cells_x - 1 : cells_x, :]
        return carry

    lax.fori_loop(0, vectors, one, 0)
    lane = lax.broadcasted_iota(jnp.int32, (8, 128), 1)
    table = table_ref[...]
    for place, number in enumerate((0, 3, 6, 2, 5, 8)):
        for b in range(vectors):
            table = jnp.where(lane == number * vectors + b, faces(rows_ref[place * vectors + b]), table)
    blocks_ref[...] = table
    width = pay_ref.shape[2]
    wide = jnp.concatenate([table, jnp.zeros((8, width - 128), F32)], axis=1)
    line = jnp.zeros((1, width), F32)
    for a in range(vectors):
        piece = wide[a : a + 1, :]
        line = line + (pltpu.roll(piece, a * SLOT, 1) if a else piece)
    for place in range(pay_ref.shape[0]):
        pay_ref[place] = line


def local_kernel(range_ref, inverse_ref, r_ref, xlo_ref, xhi_ref, ylo_ref, yhi_ref, out_ref, ext_ref, sol_ref):
    cells_x, cells_y = r_ref.shape[1:3]
    ext_x, ext_y = cells_x + 2, cells_y + 2
    half_x, half_y = ext_x // 2, ext_y // 2
    first = xlo_ref.shape[0] - 3
    halves = ((0, slice(0, 128)), (1, slice(128, 256)))
    for c in range(3):
        layers = [xlo_ref[first + c]] + [r_ref[c, x] for x in range(cells_x)] + [xhi_ref[first + c]]
        layers = [layer.astype(F32) for layer in layers]
        low, high = ylo_ref[first + c].astype(F32), yhi_ref[first + c].astype(F32)
        for h, lanes in halves:
            ext_ref[c, 0, h, 0:ext_x, :] = low[:, lanes]
            ext_ref[c, ext_y - 1, h, 0:ext_x, :] = high[:, lanes]
            for e, layer in enumerate(layers):
                for y in range(cells_y):
                    ext_ref[c, y + 1, h, e : e + 1, :] = layer[y : y + 1, lanes]
    at = lax.broadcasted_iota(jnp.int32, (half_x, r_ref.shape[3]), 0)
    for v in range(half_y):
        fields = []
        for m in range(12):
            c, s, t = m // 4, m // 2 % 2, m % 2
            e, f = 2 * at + s, 2 * v + t
            keep = (f >= range_ref[2]) & (f < range_ref[3]) & (e >= range_ref[0]) & (e < range_ref[1])
            value = jnp.concatenate([ext_ref[c, f, h, pl.ds(s, half_x, stride=2), :] for h, _ in halves], axis=1)
            fields.append(jnp.where(keep, value, 0.0))
        for i in range(12):
            acc = None
            for m in range(12):
                term = inverse_ref[i, m, v].astype(F32) * fields[m]
                acc = term if acc is None else acc + term
            c, s, t = i // 4, i // 2 % 2, i % 2
            for h, lanes in halves:
                sol_ref[c, 2 * v + t, h, pl.ds(s, half_x, stride=2), :] = acc[:, lanes]
    for c in range(3):
        for y in range(cells_y):
            for h, lanes in halves:
                for x in range(cells_x):
                    out_ref[c, x, y : y + 1, lanes] = sol_ref[c, y + 1, h, x + 1 : x + 2, :]


def moved_by(value, choice, dims):
    high = value.astype(jnp.bfloat16).astype(F32)
    middle = (value - high).astype(jnp.bfloat16).astype(F32)
    parts = jnp.concatenate([high, middle, (value - high) - middle], axis=0).astype(jnp.bfloat16)
    result = lax.dot_general(parts, choice, (dims, ((), ())), preferred_element_type=F32)
    return (result[0:8] + result[8:16]) + result[16:24]


def slots_of(packed_ref):
    count = packed_ref.shape[1]
    ids = packed_ref[73:74, :].astype(jnp.int32)
    return (lax.broadcasted_iota(jnp.int32, (count, count), 0) == ids).astype(F32).astype(jnp.bfloat16)


def share_of(vector, piece):
    line = jnp.concatenate([vector[b : b + 1, :] for b in range(8)], axis=1)
    line = jnp.broadcast_to(line, (8, line.shape[1]))
    acc = jnp.zeros(line.shape, F32)
    group = 4

    def step(t, acc):
        tiles, inner = [], []
        for q in range(group):
            tile = piece[pl.ds(pl.multiple_of((t * group + q) * 8, 8), 8), :]
            tiles.append(tile)
            inner.append(jnp.sum(tile * line, axis=1, keepdims=True))
        for tile, value in zip(tiles, inner):
            acc = acc + tile * value
        return acc

    acc = lax.fori_loop(0, piece.shape[0] // 8 // group, step, acc)
    total = jnp.sum(acc, axis=0, keepdims=True)
    blocks = vector.shape[1]
    return jnp.concatenate([total[:, b * blocks : (b + 1) * blocks] for b in range(8)], axis=0)


def first_kernel(
    n_narrow, size_z, core_ref, own_ref, other_ref, piece, packed_ref, rhs_ref, share_ref, rows_ref
):
    size_y = own_ref.shape[0]
    chips = n_narrow * size_y * size_z
    for got_ref, core in ((own_ref, core_ref[0]), (other_ref, 1 - core_ref[0])):
        for y in range(size_y):
            for x in range(n_narrow):
                place = pl.multiple_of(core * chips + (x * size_y + y) * size_z, 8)
                block = got_ref[y, x * size_z : (x + 1) * size_z]
                rows_ref[pl.ds(place, size_z), :] = block.reshape(size_z, block.shape[2])
    packed_ref[...] = rows_ref[...].T
    own = jnp.concatenate([packed_ref[a * SLOT + 72 : a * SLOT + 73, :] for a in range(8)], axis=0)
    rhs = moved_by(own, slots_of(packed_ref), ((1,), (1,)))
    rhs_ref[...] = rhs
    share = share_of(rhs, piece)
    for place in range(share_ref.shape[0]):
        share_ref[place] = share


def summed(parts_ref):
    parts = [parts_ref[k] for k in range(parts_ref.shape[0])]
    while len(parts) > 1:
        parts = [parts[k] + parts[k + 1] for k in range(0, len(parts), 2)]
    return parts[0]


def second_kernel(n_narrow, packed_ref, rhs_ref, parts_ref, piece, first_ref, share_ref):
    first = summed(parts_ref)
    first_ref[...] = first
    slots = slots_of(packed_ref)
    there = moved_by(first, slots, ((1,), (0,)))
    size = there.shape[1] // 2
    chips = size // n_narrow
    halves = [there[:, :size], there[:, size:]]
    at = lax.broadcasted_iota(jnp.int32, halves[0].shape, 1)
    row, column = at // chips, at % chips
    near = []
    for dx in (-1, 0, 1):
        for dy in (-1, 0, 1):
            sides = []
            for core in range(2):
                step = (core + dy) // 2
                move = (-(dx * chips + step)) % size
                value = halves[(core + dy) % 2]
                value = pltpu.roll(value, move, 1) if move else value
                keep = (row + dx >= 0) & (row + dx < n_narrow) & (column + step >= 0) & (column + step < chips)
                sides.append(jnp.where(keep, value, 0.0))
            near.append(jnp.concatenate(sides, axis=1))
    near.append(jnp.zeros_like(there))
    near = jnp.concatenate(near, axis=0)
    image = jnp.concatenate(
        [jnp.sum(packed_ref[a * SLOT : (a + 1) * SLOT, :] * near, axis=0, keepdims=True) for a in range(8)], axis=0
    )
    vector = rhs_ref[...] - moved_by(image, slots, ((1,), (1,)))
    share = share_of(vector, piece)
    for place in range(share_ref.shape[0]):
        share_ref[place] = share


def last_kernel(ids_ref, z_ref, local_ref, first_ref, parts_ref, out_ref, sol_ref):
    solution = first_ref[...] + summed(parts_ref)
    sol_ref[...] = solution
    at = lax.broadcasted_iota(jnp.int32, solution.shape, 1)
    weights = jnp.sum(jnp.where(at == ids_ref[4], solution, 0.0), axis=1, keepdims=True)
    for x in range(z_ref.shape[2]):
        for i in range(3):
            acc = local_ref[i, x]
            for a in range(8):
                acc = acc + weights[a : a + 1, :] * z_ref[a, i, x].astype(F32)
            out_ref[i, x] = acc


def call(kernel, out_shape, in_specs, scratch=(), flops=0, moved=0, name=None):
    return pl.pallas_call(
        kernel,
        out_shape=[jax.ShapeDtypeStruct(shape, F32) for shape in out_shape],
        in_specs=in_specs,
        out_specs=[VMEM] * len(out_shape),
        scratch_shapes=list(scratch),
        compiler_params=pltpu.CompilerParams(vmem_limit_bytes=24 * 2**20),
        cost_estimate=pl.CostEstimate(flops=flops, bytes_accessed=moved, transcendentals=0),
        name=name,
    )


def body(
    deflation,
    residual,
    stiffness,
    mass,
    stencil,
    local_inverse,
    inverse_factor,
    margin_range,
    neighbor_blocks,
):
    vectors, _, cells_x, cells_y, depth = deflation.shape
    n_narrow, size_z = lax.axis_size("narrow"), lax.axis_size("z")
    count = lax.axis_size(WIDE) * n_narrow
    n_near = n_narrow * size_z
    size_y = lax.axis_size("y")

    rounded = residual.astype(jnp.bfloat16)
    couplings = stencil.transpose(1, 2, 0)
    ids = neighbor_blocks.reshape(-1)
    ranges = margin_range.reshape(-1)

    def swaps(axis):
        size = lax.axis_size(axis)
        even = [(k, k ^ 1) for k in range(size)]
        odd = [(k, ((k + 1) ^ 1) - 1) for k in range(1, size - 1)]
        return even, odd, lax.axis_index(axis) % 2 == 0

    def exchanged(sending_low, sending_high, axis):
        even, odd, is_even = swaps(axis)

        def chosen(first, second):
            return jnp.concatenate([jnp.where(is_even, x, y) for x, y in zip(first, second)], axis=0)

        one = lax.ppermute(chosen(sending_high, sending_low), axis, even)
        two = lax.ppermute(chosen(sending_low, sending_high), axis, odd)
        return one, two, is_even

    vector_fields = deflation.reshape(3 * vectors, cells_x, cells_y, depth)
    fields = (vector_fields, rounded)
    one, two, is_even = exchanged([f[:, 0] for f in fields], [f[:, cells_x - 1] for f in fields], "narrow")

    done = vectors // 2
    zf, zy, sy, table = call(
        functools.partial(before_kernel, done),
        [(vectors, 3, cells_x, cells_y, depth), (2, vectors, 3, 8, depth), (2, 8, depth), (8, 128)],
        [SMEM, SMEM] + [VMEM] * 4,
        [pltpu.VMEM((done + 1, 8, 128), F32)],
        flops=20_000_000,
        moved=1_000_000,
        name="before",
    )(couplings, ids, deflation, rounded, stiffness, mass)
    one, two, table = lax.optimization_barrier((one, two, table))
    xlo, xhi = jnp.where(is_even, two, one), jnp.where(is_even, one, two)

    def side(y):
        middle = jnp.concatenate([f[:, :, y] for f in fields], axis=0)
        return [jnp.concatenate([xlo[:, y : y + 1], middle, xhi[:, y : y + 1]], axis=1)]

    one, two, is_even = exchanged(side(0), side(cells_y - 1), WIDE)
    ylo, yhi = jnp.where(is_even, two, one), jnp.where(is_even, one, two)

    rows = inverse_factor.shape[0]
    own = inverse_factor.reshape(rows, count, vectors).transpose(0, 2, 1).reshape(rows, count * vectors)

    held = lax.all_gather(own, ("z", "core"), tiled=True)

    (table,) = call(
        functools.partial(inner_kernel, done),
        [(8, 128)],
        [SMEM] + [VMEM] * 6,
        [pltpu.VMEM((3 * vectors, 8, 128), F32)],
        flops=30_000_000,
        moved=1_000_000,
        name="inner",
    )(couplings, zf, stiffness, mass, xlo, xhi, table)
    table, payload = call(
        outer_kernel,
        [(8, 128), (n_near, 1, SLOT * vectors)],
        [SMEM] + [VMEM] * 5,
        [pltpu.VMEM((6 * vectors, 8, 128), F32)],
        flops=10_000_000,
        moved=2_000_000,
        name="outer",
    )(couplings, table, zy, sy, ylo, yhi)
    got = lax.all_to_all(payload, ("narrow", "z"), 0, 0)
    got = lax.all_to_all(jnp.broadcast_to(got[None], (size_y,) + got.shape), "y", 0, 0)
    got, held = lax.optimization_barrier((got, held))
    other = lax.ppermute(got, "core", [(0, 1), (1, 0)])
    (local,) = call(
        local_kernel,
        [(3, cells_x, cells_y, depth)],
        [SMEM] + [VMEM] * 6,
        [pltpu.VMEM((3, cells_y + 2, 2, 8, depth // 2), F32)] * 2,
        flops=2_000_000,
        moved=3_000_000,
        name="local",
    )(ranges, local_inverse.transpose(0, 1, 3, 2, 4), rounded, xlo, xhi, ylo, yhi)

    group = ("narrow", "y")
    members = lax.axis_size(group)

    def spread(share):
        return lax.all_to_all(share, group, 0, 0)

    core = lax.axis_index("core").astype(jnp.int32).reshape(1)
    packed, rhs, share = call(
        functools.partial(first_kernel, n_narrow, size_z),
        [(SLOT * vectors, count), (vectors, count), (members, vectors, count)],
        [SMEM] + [VMEM] * 3,
        [pltpu.VMEM((count, SLOT * vectors), F32)],
        flops=2_000_000,
        moved=3_000_000,
        name="first",
    )(core, got, other, held)
    first, share = call(
        functools.partial(second_kernel, n_narrow),
        [(vectors, count), (members, vectors, count)],
        [VMEM] * 4,
        flops=2_000_000,
        moved=3_000_000,
        name="second",
    )(packed, rhs, spread(share), held)
    preconditioned, solved = call(
        last_kernel,
        [(3, cells_x, cells_y, depth), (vectors, count)],
        [SMEM] + [VMEM] * 4,
        flops=1_000_000,
        moved=1_000_000,
        name="last",
    )(ids, deflation, local, first, spread(share))
    coarse_solution = solved.T.reshape(-1)
    blocks = table[:, : 9 * vectors].reshape(vectors, 9, vectors).transpose(1, 0, 2)
    return preconditioned, blocks.reshape(1, 1, 9, vectors, vectors), coarse_solution


def solution(mesh):
    n_narrow, n_wide = mesh.devices.shape
    fine = jax.sharding.Mesh(mesh.devices.reshape(n_narrow, n_wide // 16, 8, 2), ("narrow",) + WIDE)
    placed = (
        P(None, None, "narrow", WIDE, None),
        P(None, "narrow", WIDE, None),
        P("narrow", WIDE, None),
        P("narrow", WIDE, None),
        P(),
        P(None, None, "narrow", WIDE, None),
        P(("narrow",) + WIDE, None),
        P("narrow", WIDE, None, None),
        P("narrow", WIDE, None),
    )
    return jax.shard_map(
        body,
        mesh=fine,
        in_specs=placed,
        out_specs=(P(None, "narrow", WIDE, None), P("narrow", WIDE, None, None, None), P()),
        check_vma=False,
    )
```

```python
import functools

import jax
import jax.numpy as jnp
from jax import lax
from jax.experimental import pallas as pl
from jax.experimental.pallas import tpu as pltpu
from jax.sharding import PartitionSpec as P

F32 = jnp.float32
WIDE = ("y", "z", "core")
SLOT = 80
VMEM = pl.BlockSpec(memory_space=pltpu.VMEM)
SMEM = pl.BlockSpec(memory_space=pltpu.SMEM)


def shifted(value, offset, axis):
    if offset == 0:
        return value
    size = value.shape[axis]
    rolled = pltpu.roll(value, (-offset) % size, axis)
    at = lax.broadcasted_iota(jnp.int32, value.shape, axis)
    keep = at < size - offset if offset > 0 else at >= -offset
    return jnp.where(keep, rolled, 0.0)


def rows_sum(value):
    return jnp.sum(value[:, :128] + value[:, 128:], axis=0, keepdims=True)


def entry(s_ref, ox, oy, oz, i, j):
    return s_ref[i, j, ((ox + 1) * 3 + oy + 1) * 3 + oz + 1]


def faces(total):
    return jnp.sum(total, axis=1, keepdims=True)


def halved(value):
    high = value.astype(jnp.bfloat16)
    return high, (value - high.astype(F32)).astype(jnp.bfloat16)


def laid(s_ref, out_ref, begin, rows, choices):
    value = jnp.zeros((rows, 128), F32)
    for mask, which in choices:
        value = jnp.where(mask, entry(s_ref, *which), value)
    high, low = halved(value)
    out_ref[begin : begin + rows, :128] = high
    out_ref[begin : begin + rows, 128:] = low


def matrices(s_ref, own_ref, x_ref, y_ref, cells_x, cells_y):
    rows = cells_x * cells_y
    row = lax.broadcasted_iota(jnp.int32, (rows, 128), 0)
    col = lax.broadcasted_iota(jnp.int32, (rows, 128), 1)
    dx = col // cells_y % cells_x - row // cells_y
    dy = col % cells_y - row % cells_y
    masks = []
    for j in range(3):
        for ox in (-1, 0, 1):
            for oy in (-1, 0, 1):
                masks.append((j, ox, oy, (col // rows == j) & (dx == ox) & (dy == oy)))
    for oz in (-1, 0, 1):
        for i in range(3):
            choices = [(mask, (ox, oy, oz, i, j)) for j, ox, oy, mask in masks]
            laid(s_ref, own_ref, ((oz + 1) * 3 + i) * rows, rows, choices)
    row = lax.broadcasted_iota(jnp.int32, (8, 128), 0)
    col = lax.broadcasted_iota(jnp.int32, (8, 128), 1)
    at = col % 8
    for oz in (-1, 0, 1):
        for face in range(2):
            side = 2 * face - 1
            here = [col // 8 == face * 3 + j for j in range(3)]
            for i in range(3):
                choices = [
                    (here[j] & (at - row == oy), (side, oy, oz, i, j)) for j in range(3) for oy in (-1, 0, 1)
                ]
                laid(s_ref, x_ref, (((oz + 1) * 2 + face) * 3 + i) * 8, 8, choices)
                inside = (row < cells_x) & (at >= 1) & (at <= cells_x)
                choices = [
                    (here[j] & inside & (at - 1 - row == ox), (ox, side, oz, i, j))
                    for j in range(3)
                    for ox in (-1, 0, 1)
                ]
                laid(s_ref, y_ref, ((((oz + 1) * 2 + face) * 2) * 3 + i) * 8, 8, choices)
                choices = []
                for j in range(3):
                    choices.append((here[j] & (row == 0) & (at == 0), (-1, side, oz, i, j)))
                    choices.append((here[j] & (row == cells_x - 1) & (at == cells_x + 1), (1, side, oz, i, j)))
                laid(s_ref, y_ref, ((((oz + 1) * 2 + face) * 2 + 1) * 3 + i) * 8, 8, choices)


def images(matrix, cells):
    blank = jnp.zeros((128 - cells.shape[0], cells.shape[1]), F32)
    twice = jnp.concatenate([cells, blank, cells, blank], axis=0).astype(jnp.bfloat16)
    result = jnp.dot(matrix, twice, preferred_element_type=F32)
    third = result.shape[0] // 3
    low, mid, high = result[:third], result[third : 2 * third], result[2 * third :]
    return shifted(low, -1, 1) + mid + shifted(high, 1, 1)


def before_kernel(
    s_ref, ids_ref, z_ref, r_ref, stiff_ref, zf_ref, zy_ref, sy_ref, table_ref, own_ref, x_ref, y_ref, rows_ref
):
    vectors, _, cells_x, cells_y, depth = z_ref.shape
    own_y = (0, cells_y - 1)
    blank = jnp.zeros((8 - cells_x, depth), F32)

    def columns(rows):
        return jnp.concatenate(rows + [blank], axis=0)

    matrices(s_ref, own_ref, x_ref, y_ref, cells_x, cells_y)

    def convert(a, carry):
        for i in range(3):
            cells = [z_ref[a, i, x].astype(F32) for x in range(cells_x)]
            for x in range(cells_x):
                zf_ref[a, i, x] = cells[x]
            for face, y in enumerate(own_y):
                zy_ref[face, a, i] = columns([cell[y : y + 1, :] for cell in cells])
        return carry

    lax.fori_loop(0, vectors, convert, 0)
    for face, y in enumerate(own_y):
        sy_ref[face] = columns([stiff_ref[x, y : y + 1, :] for x in range(cells_x)])
    for a in range(vectors):
        total = None
        for i in range(3):
            for x in range(cells_x):
                term = zf_ref[a, i, x] * r_ref[i, x].astype(F32)
                total = term if total is None else total + term
        rows_ref[0, a : a + 1, :] = rows_sum(total)

    lane = lax.broadcasted_iota(jnp.int32, (8, 128), 1)
    table = jnp.where(lane == 9 * vectors + 1, ids_ref[4].astype(F32), 0.0)
    table_ref[...] = jnp.where(lane == 9 * vectors, faces(rows_ref[0]), table)


def inner_kernel(
    own_ref, x_ref, zf_ref, stiff_ref, mass_ref, xlo_ref, xhi_ref, before_ref, table_ref, rows_ref
):
    vectors, _, cells_x, cells_y, depth = zf_ref.shape
    own_x = (0, cells_x - 1)

    def one(b, carry):
        cells = zf_ref[b].reshape(3 * cells_x * cells_y, depth)
        image = images(own_ref[...], cells).reshape(3, cells_x, cells_y, depth)
        weighted = [
            [stiff_ref[x] * image[i, x] + mass_ref[x] * zf_ref[b, i, x] for x in range(cells_x)] for i in range(3)
        ]
        for a in range(vectors):
            total = None
            for i in range(3):
                for x in range(cells_x):
                    term = zf_ref[a, i, x] * weighted[i][x]
                    total = term if total is None else total + term
            rows_ref[vectors + b, a : a + 1, :] = rows_sum(total)
        cells = [halo_ref[b * 3 + j].astype(F32) for halo_ref in (xlo_ref, xhi_ref) for j in range(3)]
        image = images(x_ref[...], jnp.concatenate(cells, axis=0))
        for face in range(2):
            stiff = stiff_ref[own_x[face]]
            weighted = [stiff * image[(face * 3 + i) * 8 : (face * 3 + i + 1) * 8] for i in range(3)]
            for a in range(vectors):
                total = sum(zf_ref[a, i, own_x[face]] * weighted[i] for i in range(3))
                rows_ref[2 * face * vectors + b, a : a + 1, :] = rows_sum(total)
        return carry

    lax.fori_loop(0, vectors, one, 0, unroll=4)
    lane = lax.broadcasted_iota(jnp.int32, (8, 128), 1)
    table = before_ref[...]
    for place, number in enumerate((1, 4, 7)):
        for b in range(vectors):
            table = jnp.where(lane == number * vectors + b, faces(rows_ref[place * vectors + b]), table)
    table_ref[...] = table


def outer_kernel(y_ref, table_ref, zy_ref, sy_ref, ylo_ref, yhi_ref, blocks_ref, pay_ref, rows_ref):
    vectors, depth = zy_ref.shape[1], zy_ref.shape[4]
    cells_x = ylo_ref.shape[1] - 2
    pad = jnp.zeros((8 - ylo_ref.shape[1], depth), F32)

    def one(b, carry):
        cells = []
        for halo_ref in (ylo_ref, yhi_ref):
            for j in range(3):
                cells += [halo_ref[b * 3 + j].astype(F32), pad]
        image = images(y_ref[...], jnp.concatenate(cells, axis=0))
        for face in range(2):
            stiff = sy_ref[face]
            begin = face * 6
            inner = [stiff * image[(begin + i) * 8 : (begin + i + 1) * 8] for i in range(3)]
            outer = [stiff * image[(begin + 3 + i) * 8 : (begin + 4 + i) * 8] for i in range(3)]
            for a in range(vectors):
                own = [zy_ref[face, a, i] for i in range(3)]
                total = sum(own[i] * inner[i] for i in range(3))
                rows_ref[(3 * face + 1) * vectors + b, a : a + 1, :] = rows_sum(total)
                total = sum(own[i] * outer[i] for i in range(3))
                half = total[:, :128] + total[:, 128:]
                rows_ref[3 * face * vectors + b, a : a + 1, :] = half[0:1, :]
                rows_ref[(3 * face + 2) * vectors + b, a : a + 1, :] = half[cells_x - 1 : cells_x, :]
        return carry

    lax.fori_loop(0, vectors, one, 0, unroll=8)
    lane = lax.broadcasted_iota(jnp.int32, (8, 128), 1)
    table = table_ref[...]
    for place, number in enumerate((0, 3, 6, 2, 5, 8)):
        for b in range(vectors):
            table = jnp.where(lane == number * vectors + b, faces(rows_ref[place * vectors + b]), table)
    blocks_ref[...] = table
    width = pay_ref.shape[2]
    wide = jnp.concatenate([table, jnp.zeros((8, width - 128), F32)], axis=1)
    line = jnp.zeros((1, width), F32)
    for a in range(vectors):
        piece = wide[a : a + 1, :]
        line = line + (pltpu.roll(piece, a * SLOT, 1) if a else piece)
    for place in range(pay_ref.shape[0]):
        pay_ref[place] = line


def local_kernel(range_ref, inverse_ref, r_ref, xlo_ref, xhi_ref, ylo_ref, yhi_ref, out_ref, ext_ref, sol_ref):
    cells_x, cells_y = r_ref.shape[1:3]
    ext_x, ext_y = cells_x + 2, cells_y + 2
    half_x, half_y = ext_x // 2, ext_y // 2
    first = xlo_ref.shape[0] - 3
    halves = ((0, slice(0, 128)), (1, slice(128, 256)))
    for c in range(3):
        layers = [xlo_ref[first + c]] + [r_ref[c, x] for x in range(cells_x)] + [xhi_ref[first + c]]
        layers = [layer.astype(F32) for layer in layers]
        low, high = ylo_ref[first + c].astype(F32), yhi_ref[first + c].astype(F32)
        for h, lanes in halves:
            ext_ref[c, 0, h, 0:ext_x, :] = low[:, lanes]
            ext_ref[c, ext_y - 1, h, 0:ext_x, :] = high[:, lanes]
            for e, layer in enumerate(layers):
                for y in range(cells_y):
                    ext_ref[c, y + 1, h, e : e + 1, :] = layer[y : y + 1, lanes]
    at = lax.broadcasted_iota(jnp.int32, (half_x, r_ref.shape[3]), 0)
    for v in range(half_y):
        fields = []
        for m in range(12):
            c, s, t = m // 4, m // 2 % 2, m % 2
            e, f = 2 * at + s, 2 * v + t
            keep = (f >= range_ref[2]) & (f < range_ref[3]) & (e >= range_ref[0]) & (e < range_ref[1])
            value = jnp.concatenate([ext_ref[c, f, h, pl.ds(s, half_x, stride=2), :] for h, _ in halves], axis=1)
            fields.append(jnp.where(keep, value, 0.0))
        for i in range(12):
            acc = None
            for m in range(12):
                term = inverse_ref[i, m, v].astype(F32) * fields[m]
                acc = term if acc is None else acc + term
            c, s, t = i // 4, i // 2 % 2, i % 2
            for h, lanes in halves:
                sol_ref[c, 2 * v + t, h, pl.ds(s, half_x, stride=2), :] = acc[:, lanes]
    for c in range(3):
        for y in range(cells_y):
            for h, lanes in halves:
                for x in range(cells_x):
                    out_ref[c, x, y : y + 1, lanes] = sol_ref[c, y + 1, h, x + 1 : x + 2, :]


def moved_by(value, choice, dims):
    high = value.astype(jnp.bfloat16).astype(F32)
    middle = (value - high).astype(jnp.bfloat16).astype(F32)
    parts = jnp.concatenate([high, middle, (value - high) - middle], axis=0).astype(jnp.bfloat16)
    result = lax.dot_general(parts, choice, (dims, ((), ())), preferred_element_type=F32)
    return (result[0:8] + result[8:16]) + result[16:24]


def lines_of(flat):
    size = flat.shape[0]
    return jnp.concatenate([jnp.broadcast_to(flat[q : q + 1, :], (8, 128)) for q in range(size)], axis=1)


def flat_of(by_vector):
    at = lax.broadcasted_iota(jnp.int32, by_vector.shape, 1)
    row = lax.broadcasted_iota(jnp.int32, by_vector.shape, 0)
    line = jnp.sum(jnp.where(at % 8 == row, by_vector, 0.0), axis=0, keepdims=True)
    return folded(line)


def folded(line):
    return jnp.concatenate([line[:, q * 128 : (q + 1) * 128] for q in range(line.shape[1] // 128)], axis=0)


def share_of(flat, pieces):
    line = lines_of(flat)
    acc = jnp.zeros(line.shape, F32)
    group = 4
    for piece in pieces:

        def step(t, acc, piece=piece):
            tiles, inner = [], []
            for q in range(group):
                tile = piece[pl.ds(pl.multiple_of((t * group + q) * 8, 8), 8), :]
                tiles.append(tile)
                inner.append(jnp.sum(tile * line, axis=1, keepdims=True))
            for tile, value in zip(tiles, inner):
                acc = acc + tile * value
            return acc

        acc = lax.fori_loop(0, piece.shape[0] // 8 // group, step, acc)
    return folded(jnp.sum(acc, axis=0, keepdims=True))


def gathered_kernel(
    n_narrow, size_z, core_ref, own_ref, other_ref, packed_ref, slots_ref, rhs_ref, rows_ref
):
    size_y = own_ref.shape[0]
    chips = n_narrow * size_y * size_z
    for got_ref, core in ((own_ref, core_ref[0]), (other_ref, 1 - core_ref[0])):
        for y in range(size_y):
            for x in range(n_narrow):
                place = pl.multiple_of(core * chips + (x * size_y + y) * size_z, 8)
                block = got_ref[y, x * size_z : (x + 1) * size_z]
                rows_ref[pl.ds(place, size_z), :] = block.reshape(size_z, block.shape[2])
    rows = rows_ref[...]
    ids = jnp.broadcast_to(rows[:, 73:74].astype(jnp.int32), slots_ref.shape)
    at = lax.broadcasted_iota(jnp.int32, slots_ref.shape, 1)
    slots_ref[...] = (at // 8 == ids).astype(F32).astype(jnp.bfloat16)
    packed = rows.T
    packed_ref[...] = packed
    own = jnp.concatenate([packed[a * SLOT + 72 : a * SLOT + 73, :] for a in range(8)], axis=0)
    rhs_ref[...] = flat_of(moved_by(own, slots_ref[...], ((1,), (0,))))


def first_kernel(rhs_ref, own_ref, other_ref, share_ref):
    share = share_of(rhs_ref[...], (own_ref, other_ref))
    for place in range(share_ref.shape[0]):
        share_ref[place] = share


def summed(parts_ref):
    parts = [parts_ref[k] for k in range(parts_ref.shape[0])]
    while len(parts) > 1:
        parts = [parts[k] + parts[k + 1] for k in range(0, len(parts), 2)]
    return parts[0]


def second_kernel(
    n_narrow, packed_ref, slots_ref, rhs_ref, parts_ref, own_ref, other_ref, first_ref, share_ref
):
    first = summed(parts_ref)
    first_ref[...] = first
    lines = lines_of(first)
    at = lax.broadcasted_iota(jnp.int32, lines.shape, 1)
    entry_at = lax.broadcasted_iota(jnp.int32, lines.shape, 0)
    lines = jnp.where(at % 8 == entry_at, lines, 0.0)
    there = moved_by(lines, slots_ref[...], ((1,), (1,)))
    size = there.shape[1] // 2
    chips = size // n_narrow
    halves = [there[:, :size], there[:, size:]]
    at = lax.broadcasted_iota(jnp.int32, halves[0].shape, 1)
    row, column = at // chips, at % chips
    near = []
    for dx in (-1, 0, 1):
        for dy in (-1, 0, 1):
            sides = []
            for core in range(2):
                step = (core + dy) // 2
                move = (-(dx * chips + step)) % size
                value = halves[(core + dy) % 2]
                value = pltpu.roll(value, move, 1) if move else value
                keep = (row + dx >= 0) & (row + dx < n_narrow) & (column + step >= 0) & (column + step < chips)
                sides.append(jnp.where(keep, value, 0.0))
            near.append(jnp.concatenate(sides, axis=1))
    near.append(jnp.zeros_like(there))
    near = jnp.concatenate(near, axis=0)
    image = jnp.concatenate(
        [jnp.sum(packed_ref[a * SLOT : (a + 1) * SLOT, :] * near, axis=0, keepdims=True) for a in range(8)], axis=0
    )
    vector = rhs_ref[...] - flat_of(moved_by(image, slots_ref[...], ((1,), (0,))))
    share = share_of(vector, (own_ref, other_ref))
    for place in range(share_ref.shape[0]):
        share_ref[place] = share


def last_kernel(ids_ref, z_ref, local_ref, first_ref, parts_ref, out_ref, sol_ref):
    solution = first_ref[...] + summed(parts_ref)
    sol_ref[...] = solution
    lines = lines_of(solution)
    at = lax.broadcasted_iota(jnp.int32, lines.shape, 1)
    row = lax.broadcasted_iota(jnp.int32, lines.shape, 0)
    weights = jnp.sum(jnp.where(at == ids_ref[4] * 8 + row, lines, 0.0), axis=1, keepdims=True)
    for x in range(z_ref.shape[2]):
        for i in range(3):
            acc = local_ref[i, x]
            for a in range(8):
                acc = acc + weights[a : a + 1, :] * z_ref[a, i, x].astype(F32)
            out_ref[i, x] = acc


def call(kernel, out_shape, in_specs, scratch=(), flops=0, moved=0, name=None):
    return pl.pallas_call(
        kernel,
        out_shape=[
            shape if isinstance(shape, jax.ShapeDtypeStruct) else jax.ShapeDtypeStruct(shape, F32) for shape in out_shape
        ],
        in_specs=in_specs,
        out_specs=[VMEM] * len(out_shape),
        scratch_shapes=list(scratch),
        compiler_params=pltpu.CompilerParams(vmem_limit_bytes=24 * 2**20),
        cost_estimate=pl.CostEstimate(flops=flops, bytes_accessed=moved, transcendentals=0),
        name=name,
    )


def body(
    deflation,
    residual,
    stiffness,
    mass,
    stencil,
    local_inverse,
    inverse_factor,
    margin_range,
    neighbor_blocks,
):
    vectors, _, cells_x, cells_y, depth = deflation.shape
    n_narrow, size_z = lax.axis_size("narrow"), lax.axis_size("z")
    count = lax.axis_size(WIDE) * n_narrow
    n_near = n_narrow * size_z
    size_y = lax.axis_size("y")

    rounded = residual.astype(jnp.bfloat16)
    couplings = stencil.transpose(1, 2, 0)
    ids = neighbor_blocks.reshape(-1)
    ranges = margin_range.reshape(-1)

    def swaps(axis):
        size = lax.axis_size(axis)
        even = [(k, k ^ 1) for k in range(size)]
        odd = [(k, ((k + 1) ^ 1) - 1) for k in range(1, size - 1)]
        return even, odd, lax.axis_index(axis) % 2 == 0

    def exchanged(sending_low, sending_high, axis):
        even, odd, is_even = swaps(axis)

        def chosen(first, second):
            return jnp.concatenate([jnp.where(is_even, x, y) for x, y in zip(first, second)], axis=0)

        one = lax.ppermute(chosen(sending_high, sending_low), axis, even)
        two = lax.ppermute(chosen(sending_low, sending_high), axis, odd)
        return one, two, is_even

    vector_fields = deflation.reshape(3 * vectors, cells_x, cells_y, depth)
    fields = (vector_fields, rounded)
    one, two, is_even = exchanged([f[:, 0] for f in fields], [f[:, cells_x - 1] for f in fields], "narrow")

    def matrix(rows):
        return jax.ShapeDtypeStruct((rows, 256), jnp.bfloat16)

    zf, zy, sy, table, own_matrix, x_matrix, y_matrix = call(
        before_kernel,
        [
            (vectors, 3, cells_x, cells_y, depth),
            (2, vectors, 3, 8, depth),
            (2, 8, depth),
            (8, 128),
            matrix(9 * cells_x * cells_y),
            matrix(144),
            matrix(288),
        ],
        [SMEM, SMEM] + [VMEM] * 3,
        [pltpu.VMEM((1, 8, 128), F32)],
        flops=20_000_000,
        moved=1_000_000,
        name="before",
    )(couplings, ids, deflation, rounded, stiffness)
    def joined(rows, partner):
        return jnp.concatenate([rows, lax.ppermute(rows, "z", [(k, partner(k) % size_z) for k in range(size_z)])], axis=0)

    rows_z = joined(inverse_factor, lambda k: k ^ 1)
    one, two, table, rows_z = lax.optimization_barrier((one, two, table, rows_z))
    rows_z = joined(rows_z, lambda k: k ^ 2)
    xlo, xhi = jnp.where(is_even, two, one), jnp.where(is_even, one, two)

    def side(y):
        middle = jnp.concatenate([f[:, :, y] for f in fields], axis=0)
        return [jnp.concatenate([xlo[:, y : y + 1], middle, xhi[:, y : y + 1]], axis=1)]

    one, two, is_even = exchanged(side(0), side(cells_y - 1), WIDE)
    ylo, yhi = jnp.where(is_even, two, one), jnp.where(is_even, one, two)

    (table,) = call(
        inner_kernel,
        [(8, 128)],
        [VMEM] * 8,
        [pltpu.VMEM((3 * vectors, 8, 128), F32)],
        flops=10_000_000,
        moved=1_000_000,
        name="inner",
    )(own_matrix, x_matrix, zf, stiffness, mass, xlo, xhi, table)
    table, rows_z = lax.optimization_barrier((table, rows_z))
    rows_z = joined(rows_z, lambda k: k + 2 if k // 2 % 2 else k - 2)
    table, payload = call(
        outer_kernel,
        [(8, 128), (n_near, 1, SLOT * vectors)],
        [VMEM] * 6,
        [pltpu.VMEM((6 * vectors, 8, 128), F32)],
        flops=10_000_000,
        moved=2_000_000,
        name="outer",
    )(y_matrix, table, zy, sy, ylo, yhi)
    got = lax.all_to_all(payload, ("narrow", "z"), 0, 0)
    got = lax.all_to_all(jnp.broadcast_to(got[None], (size_y,) + got.shape), "y", 0, 0)
    got, rows_z = lax.optimization_barrier((got, rows_z))
    other = lax.ppermute(got, "core", [(0, 1), (1, 0)])
    held = [rows_z, lax.ppermute(rows_z, "core", [(0, 1), (1, 0)])]
    (local,) = call(
        local_kernel,
        [(3, cells_x, cells_y, depth)],
        [SMEM] + [VMEM] * 6,
        [pltpu.VMEM((3, cells_y + 2, 2, 8, depth // 2), F32)] * 2,
        flops=2_000_000,
        moved=3_000_000,
        name="local",
    )(ranges, local_inverse.transpose(0, 1, 3, 2, 4), rounded, xlo, xhi, ylo, yhi)

    group = ("narrow", "y")
    members = lax.axis_size(group)

    def spread(share):
        return lax.all_to_all(share, group, 0, 0)

    core = lax.axis_index("core").astype(jnp.int32).reshape(1)
    flat = (count * vectors // 128, 128)
    packed, slots, rhs = call(
        functools.partial(gathered_kernel, n_narrow, size_z),
        [(SLOT * vectors, count), jax.ShapeDtypeStruct((count, count * vectors), jnp.bfloat16), flat],
        [SMEM] + [VMEM] * 2,
        [pltpu.VMEM((count, SLOT * vectors), F32)],
        flops=2_000_000,
        moved=12_000_000,
        name="gathered",
    )(core, got, other)
    (share,) = call(
        first_kernel,
        [(members,) + flat],
        [VMEM] * 3,
        flops=2_000_000,
        moved=2_000_000,
        name="first",
    )(rhs, *held)
    first, share = call(
        functools.partial(second_kernel, n_narrow),
        [flat, (members,) + flat],
        [VMEM] * 6,
        flops=2_000_000,
        moved=3_000_000,
        name="second",
    )(packed, slots, rhs, spread(share), *held)
    preconditioned, solved = call(
        last_kernel,
        [(3, cells_x, cells_y, depth), flat],
        [SMEM] + [VMEM] * 4,
        flops=1_000_000,
        moved=1_000_000,
        name="last",
    )(ids, deflation, local, first, spread(share))
    coarse_solution = solved.reshape(-1)
    blocks = table[:, : 9 * vectors].reshape(vectors, 9, vectors).transpose(1, 0, 2)
    return preconditioned, blocks.reshape(1, 1, 9, vectors, vectors), coarse_solution


def solution(mesh):
    n_narrow, n_wide = mesh.devices.shape
    fine = jax.sharding.Mesh(mesh.devices.reshape(n_narrow, n_wide // 16, 8, 2), ("narrow",) + WIDE)
    placed = (
        P(None, None, "narrow", WIDE, None),
        P(None, "narrow", WIDE, None),
        P("narrow", WIDE, None),
        P("narrow", WIDE, None),
        P(),
        P(None, None, "narrow", WIDE, None),
        P(("narrow",) + WIDE, None),
        P("narrow", WIDE, None, None),
        P("narrow", WIDE, None),
    )
    return jax.shard_map(
        body,
        mesh=fine,
        in_specs=placed,
        out_specs=(P(None, "narrow", WIDE, None), P("narrow", WIDE, None, None, None), P()),
        check_vma=False,
    )
```

```python
import functools

import jax
import jax.numpy as jnp
from jax import lax
from jax.experimental import pallas as pl
from jax.experimental.pallas import tpu as pltpu
from jax.sharding import PartitionSpec as P

F32 = jnp.float32
WIDE = ("y", "z", "core")
SLOT = 80
VMEM = pl.BlockSpec(memory_space=pltpu.VMEM)
SMEM = pl.BlockSpec(memory_space=pltpu.SMEM)


def shifted(value, offset, axis):
    if offset == 0:
        return value
    size = value.shape[axis]
    rolled = pltpu.roll(value, (-offset) % size, axis)
    at = lax.broadcasted_iota(jnp.int32, value.shape, axis)
    keep = at < size - offset if offset > 0 else at >= -offset
    return jnp.where(keep, rolled, 0.0)


def rows_sum(value):
    return jnp.sum(value[:, :128] + value[:, 128:], axis=0, keepdims=True)


def entry(s_ref, ox, oy, oz, i, j):
    return s_ref[i, j, ((ox + 1) * 3 + oy + 1) * 3 + oz + 1]


def faces(total):
    return jnp.sum(total, axis=1, keepdims=True)


def halved(value):
    high = value.astype(jnp.bfloat16)
    return high, (value - high.astype(F32)).astype(jnp.bfloat16)


def laid(s_ref, out_ref, begin, rows, choices):
    value = jnp.zeros((rows, 128), F32)
    for mask, which in choices:
        value = jnp.where(mask, entry(s_ref, *which), value)
    high, low = halved(value)
    out_ref[begin : begin + rows, :128] = high
    out_ref[begin : begin + rows, 128:] = low


def matrices(s_ref, own_ref, x_ref, y_ref, cells_x, cells_y):
    rows = cells_x * cells_y
    row = lax.broadcasted_iota(jnp.int32, (rows, 128), 0)
    col = lax.broadcasted_iota(jnp.int32, (rows, 128), 1)
    dx = col // cells_y % cells_x - row // cells_y
    dy = col % cells_y - row % cells_y
    masks = []
    for j in range(3):
        for ox in (-1, 0, 1):
            for oy in (-1, 0, 1):
                masks.append((j, ox, oy, (col // rows == j) & (dx == ox) & (dy == oy)))
    for oz in (-1, 0, 1):
        for i in range(3):
            choices = [(mask, (ox, oy, oz, i, j)) for j, ox, oy, mask in masks]
            laid(s_ref, own_ref, ((oz + 1) * 3 + i) * rows, rows, choices)
    row = lax.broadcasted_iota(jnp.int32, (8, 128), 0)
    col = lax.broadcasted_iota(jnp.int32, (8, 128), 1)
    at = col % 8
    for oz in (-1, 0, 1):
        for face in range(2):
            side = 2 * face - 1
            here = [col // 8 == face * 3 + j for j in range(3)]
            for i in range(3):
                choices = [
                    (here[j] & (at - row == oy), (side, oy, oz, i, j)) for j in range(3) for oy in (-1, 0, 1)
                ]
                laid(s_ref, x_ref, (((oz + 1) * 2 + face) * 3 + i) * 8, 8, choices)
                inside = (row < cells_x) & (at >= 1) & (at <= cells_x)
                choices = [
                    (here[j] & inside & (at - 1 - row == ox), (ox, side, oz, i, j))
                    for j in range(3)
                    for ox in (-1, 0, 1)
                ]
                laid(s_ref, y_ref, ((((oz + 1) * 2 + face) * 2) * 3 + i) * 8, 8, choices)
                choices = []
                for j in range(3):
                    choices.append((here[j] & (row == 0) & (at == 0), (-1, side, oz, i, j)))
                    choices.append((here[j] & (row == cells_x - 1) & (at == cells_x + 1), (1, side, oz, i, j)))
                laid(s_ref, y_ref, ((((oz + 1) * 2 + face) * 2 + 1) * 3 + i) * 8, 8, choices)


def images(matrix, cells):
    blank = jnp.zeros((128 - cells.shape[0], cells.shape[1]), F32)
    twice = jnp.concatenate([cells, blank, cells, blank], axis=0).astype(jnp.bfloat16)
    result = jnp.dot(matrix, twice, preferred_element_type=F32)
    third = result.shape[0] // 3
    low, mid, high = result[:third], result[third : 2 * third], result[2 * third :]
    return shifted(low, -1, 1) + mid + shifted(high, 1, 1)


def before_kernel(
    s_ref, ids_ref, z_ref, r_ref, stiff_ref, zf_ref, zy_ref, sy_ref, table_ref, own_ref, x_ref, y_ref, rows_ref
):
    vectors, _, cells_x, cells_y, depth = z_ref.shape
    own_y = (0, cells_y - 1)
    blank = jnp.zeros((8 - cells_x, depth), F32)

    def columns(rows):
        return jnp.concatenate(rows + [blank], axis=0)

    matrices(s_ref, own_ref, x_ref, y_ref, cells_x, cells_y)

    def convert(a, carry):
        for i in range(3):
            cells = [z_ref[a, i, x].astype(F32) for x in range(cells_x)]
            for x in range(cells_x):
                zf_ref[a, i, x] = cells[x]
            for face, y in enumerate(own_y):
                zy_ref[face, a, i] = columns([cell[y : y + 1, :] for cell in cells])
        return carry

    lax.fori_loop(0, vectors, convert, 0)
    for face, y in enumerate(own_y):
        sy_ref[face] = columns([stiff_ref[x, y : y + 1, :] for x in range(cells_x)])
    for a in range(vectors):
        total = None
        for i in range(3):
            for x in range(cells_x):
                term = zf_ref[a, i, x] * r_ref[i, x].astype(F32)
                total = term if total is None else total + term
        rows_ref[0, a : a + 1, :] = rows_sum(total)

    lane = lax.broadcasted_iota(jnp.int32, (8, 128), 1)
    table = jnp.where(lane == 9 * vectors + 1, ids_ref[4].astype(F32), 0.0)
    table_ref[...] = jnp.where(lane == 9 * vectors, faces(rows_ref[0]), table)


def inner_kernel(
    own_ref, x_ref, zf_ref, stiff_ref, mass_ref, xlo_ref, xhi_ref, before_ref, table_ref, rows_ref
):
    vectors, _, cells_x, cells_y, depth = zf_ref.shape
    own_x = (0, cells_x - 1)

    def one(b, carry):
        cells = zf_ref[b].reshape(3 * cells_x * cells_y, depth)
        image = images(own_ref[...], cells).reshape(3, cells_x, cells_y, depth)
        weighted = [
            [stiff_ref[x] * image[i, x] + mass_ref[x] * zf_ref[b, i, x] for x in range(cells_x)] for i in range(3)
        ]
        for a in range(vectors):
            total = None
            for i in range(3):
                for x in range(cells_x):
                    term = zf_ref[a, i, x] * weighted[i][x]
                    total = term if total is None else total + term
            rows_ref[vectors + b, a : a + 1, :] = rows_sum(total)
        cells = [halo_ref[b * 3 + j].astype(F32) for halo_ref in (xlo_ref, xhi_ref) for j in range(3)]
        image = images(x_ref[...], jnp.concatenate(cells, axis=0))
        for face in range(2):
            stiff = stiff_ref[own_x[face]]
            weighted = [stiff * image[(face * 3 + i) * 8 : (face * 3 + i + 1) * 8] for i in range(3)]
            for a in range(vectors):
                total = sum(zf_ref[a, i, own_x[face]] * weighted[i] for i in range(3))
                rows_ref[2 * face * vectors + b, a : a + 1, :] = rows_sum(total)
        return carry

    lax.fori_loop(0, vectors, one, 0, unroll=4)
    lane = lax.broadcasted_iota(jnp.int32, (8, 128), 1)
    table = before_ref[...]
    for place, number in enumerate((1, 4, 7)):
        for b in range(vectors):
            table = jnp.where(lane == number * vectors + b, faces(rows_ref[place * vectors + b]), table)
    table_ref[...] = table


def outer_kernel(y_ref, table_ref, zy_ref, sy_ref, ylo_ref, yhi_ref, blocks_ref, pay_ref, rows_ref):
    vectors, depth = zy_ref.shape[1], zy_ref.shape[4]
    cells_x = ylo_ref.shape[1] - 2
    pad = jnp.zeros((8 - ylo_ref.shape[1], depth), F32)

    def one(b, carry):
        cells = []
        for halo_ref in (ylo_ref, yhi_ref):
            for j in range(3):
                cells += [halo_ref[b * 3 + j].astype(F32), pad]
        image = images(y_ref[...], jnp.concatenate(cells, axis=0))
        for face in range(2):
            stiff = sy_ref[face]
            begin = face * 6
            inner = [stiff * image[(begin + i) * 8 : (begin + i + 1) * 8] for i in range(3)]
            outer = [stiff * image[(begin + 3 + i) * 8 : (begin + 4 + i) * 8] for i in range(3)]
            for a in range(vectors):
                own = [zy_ref[face, a, i] for i in range(3)]
                total = sum(own[i] * inner[i] for i in range(3))
                rows_ref[(3 * face + 1) * vectors + b, a : a + 1, :] = rows_sum(total)
                total = sum(own[i] * outer[i] for i in range(3))
                half = total[:, :128] + total[:, 128:]
                rows_ref[3 * face * vectors + b, a : a + 1, :] = half[0:1, :]
                rows_ref[(3 * face + 2) * vectors + b, a : a + 1, :] = half[cells_x - 1 : cells_x, :]
        return carry

    lax.fori_loop(0, vectors, one, 0, unroll=8)
    lane = lax.broadcasted_iota(jnp.int32, (8, 128), 1)
    table = table_ref[...]
    for place, number in enumerate((0, 3, 6, 2, 5, 8)):
        for b in range(vectors):
            table = jnp.where(lane == number * vectors + b, faces(rows_ref[place * vectors + b]), table)
    blocks_ref[...] = table
    width = pay_ref.shape[2]
    wide = jnp.concatenate([table, jnp.zeros((8, width - 128), F32)], axis=1)
    line = jnp.zeros((1, width), F32)
    for a in range(vectors):
        piece = wide[a : a + 1, :]
        line = line + (pltpu.roll(piece, a * SLOT, 1) if a else piece)
    for place in range(pay_ref.shape[0]):
        pay_ref[place] = line


def local_kernel(range_ref, inverse_ref, r_ref, xlo_ref, xhi_ref, ylo_ref, yhi_ref, out_ref, ext_ref, sol_ref):
    cells_x, cells_y = r_ref.shape[1:3]
    ext_x, ext_y = cells_x + 2, cells_y + 2
    half_x, half_y = ext_x // 2, ext_y // 2
    first = xlo_ref.shape[0] - 3
    halves = ((0, slice(0, 128)), (1, slice(128, 256)))
    for c in range(3):
        layers = [xlo_ref[first + c]] + [r_ref[c, x] for x in range(cells_x)] + [xhi_ref[first + c]]
        layers = [layer.astype(F32) for layer in layers]
        low, high = ylo_ref[first + c].astype(F32), yhi_ref[first + c].astype(F32)
        for h, lanes in halves:
            ext_ref[c, 0, h, 0:ext_x, :] = low[:, lanes]
            ext_ref[c, ext_y - 1, h, 0:ext_x, :] = high[:, lanes]
            for e, layer in enumerate(layers):
                for y in range(cells_y):
                    ext_ref[c, y + 1, h, e : e + 1, :] = layer[y : y + 1, lanes]
    at = lax.broadcasted_iota(jnp.int32, (half_x, r_ref.shape[3]), 0)
    for v in range(half_y):
        fields = []
        for m in range(12):
            c, s, t = m // 4, m // 2 % 2, m % 2
            e, f = 2 * at + s, 2 * v + t
            keep = (f >= range_ref[2]) & (f < range_ref[3]) & (e >= range_ref[0]) & (e < range_ref[1])
            value = jnp.concatenate([ext_ref[c, f, h, pl.ds(s, half_x, stride=2), :] for h, _ in halves], axis=1)
            fields.append(jnp.where(keep, value, 0.0))
        for i in range(12):
            acc = None
            for m in range(12):
                term = inverse_ref[i, m, v].astype(F32) * fields[m]
                acc = term if acc is None else acc + term
            c, s, t = i // 4, i // 2 % 2, i % 2
            for h, lanes in halves:
                sol_ref[c, 2 * v + t, h, pl.ds(s, half_x, stride=2), :] = acc[:, lanes]
    for c in range(3):
        for y in range(cells_y):
            for h, lanes in halves:
                for x in range(cells_x):
                    out_ref[c, x, y : y + 1, lanes] = sol_ref[c, y + 1, h, x + 1 : x + 2, :]


def moved_by(value, choice, dims):
    high = value.astype(jnp.bfloat16).astype(F32)
    middle = (value - high).astype(jnp.bfloat16).astype(F32)
    parts = jnp.concatenate([high, middle, (value - high) - middle], axis=0).astype(jnp.bfloat16)
    result = lax.dot_general(parts, choice, (dims, ((), ())), preferred_element_type=F32)
    return (result[0:8] + result[8:16]) + result[16:24]


def lines_of(flat):
    size = flat.shape[0]
    return jnp.concatenate([jnp.broadcast_to(flat[q : q + 1, :], (8, 128)) for q in range(size)], axis=1)


def flat_of(by_vector):
    at = lax.broadcasted_iota(jnp.int32, by_vector.shape, 1)
    row = lax.broadcasted_iota(jnp.int32, by_vector.shape, 0)
    line = jnp.sum(jnp.where(at % 8 == row, by_vector, 0.0), axis=0, keepdims=True)
    return folded(line)


def folded(line):
    return jnp.concatenate([line[:, q * 128 : (q + 1) * 128] for q in range(line.shape[1] // 128)], axis=0)


def share_of(flat, pieces):
    line = lines_of(flat)
    acc = jnp.zeros(line.shape, F32)
    group = 4
    for piece in pieces:

        def step(t, acc, piece=piece):
            tiles, inner = [], []
            for q in range(group):
                tile = piece[pl.ds(pl.multiple_of((t * group + q) * 8, 8), 8), :]
                tiles.append(tile)
                inner.append(jnp.sum(tile * line, axis=1, keepdims=True))
            for tile, value in zip(tiles, inner):
                acc = acc + tile * value
            return acc

        acc = lax.fori_loop(0, piece.shape[0] // 8 // group, step, acc)
    return folded(jnp.sum(acc, axis=0, keepdims=True))


def first_kernel(
    n_narrow, size_z, place_ref, own_ref, other_ref, held_ref, held_other_ref, packed_ref, slots_ref, rhs_ref, share_ref, rows_ref
):
    size_y = own_ref.shape[0]
    chips = n_narrow * size_y * size_z
    for got_ref, core in ((own_ref, place_ref[size_y]), (other_ref, 1 - place_ref[size_y])):
        for y in range(size_y):
            for x in range(n_narrow):
                place = pl.multiple_of(core * chips + (x * size_y + place_ref[y]) * size_z, 8)
                block = got_ref[y, x * size_z : (x + 1) * size_z]
                rows_ref[pl.ds(place, size_z), :] = block.reshape(size_z, block.shape[2])
    rows = rows_ref[...]
    ids = jnp.broadcast_to(rows[:, 73:74].astype(jnp.int32), slots_ref.shape)
    at = lax.broadcasted_iota(jnp.int32, slots_ref.shape, 1)
    slots_ref[...] = (at // 8 == ids).astype(F32).astype(jnp.bfloat16)
    packed = rows.T
    packed_ref[...] = packed
    own = jnp.concatenate([packed[a * SLOT + 72 : a * SLOT + 73, :] for a in range(8)], axis=0)
    rhs = flat_of(moved_by(own, slots_ref[...], ((1,), (0,))))
    rhs_ref[...] = rhs
    share = share_of(rhs, (held_ref, held_other_ref))
    for place in range(share_ref.shape[0]):
        share_ref[place] = share


def summed(parts_ref):
    parts = [parts_ref[k] for k in range(parts_ref.shape[0])]
    while len(parts) > 1:
        parts = [parts[k] + parts[k + 1] for k in range(0, len(parts), 2)]
    return parts[0]


def second_kernel(
    n_narrow, packed_ref, slots_ref, rhs_ref, parts_ref, own_ref, other_ref, first_ref, share_ref
):
    first = summed(parts_ref)
    first_ref[...] = first
    lines = lines_of(first)
    at = lax.broadcasted_iota(jnp.int32, lines.shape, 1)
    entry_at = lax.broadcasted_iota(jnp.int32, lines.shape, 0)
    lines = jnp.where(at % 8 == entry_at, lines, 0.0)
    there = moved_by(lines, slots_ref[...], ((1,), (1,)))
    size = there.shape[1] // 2
    chips = size // n_narrow
    halves = [there[:, :size], there[:, size:]]
    at = lax.broadcasted_iota(jnp.int32, halves[0].shape, 1)
    row, column = at // chips, at % chips
    near = []
    for dx in (-1, 0, 1):
        for dy in (-1, 0, 1):
            sides = []
            for core in range(2):
                step = (core + dy) // 2
                move = (-(dx * chips + step)) % size
                value = halves[(core + dy) % 2]
                value = pltpu.roll(value, move, 1) if move else value
                keep = (row + dx >= 0) & (row + dx < n_narrow) & (column + step >= 0) & (column + step < chips)
                sides.append(jnp.where(keep, value, 0.0))
            near.append(jnp.concatenate(sides, axis=1))
    near.append(jnp.zeros_like(there))
    near = jnp.concatenate(near, axis=0)
    image = jnp.concatenate(
        [jnp.sum(packed_ref[a * SLOT : (a + 1) * SLOT, :] * near, axis=0, keepdims=True) for a in range(8)], axis=0
    )
    vector = rhs_ref[...] - flat_of(moved_by(image, slots_ref[...], ((1,), (0,))))
    share = share_of(vector, (own_ref, other_ref))
    for place in range(share_ref.shape[0]):
        share_ref[place] = share


def last_kernel(ids_ref, z_ref, local_ref, first_ref, parts_ref, out_ref, sol_ref):
    solution = first_ref[...] + summed(parts_ref)
    sol_ref[...] = solution
    lines = lines_of(solution)
    at = lax.broadcasted_iota(jnp.int32, lines.shape, 1)
    row = lax.broadcasted_iota(jnp.int32, lines.shape, 0)
    weights = jnp.sum(jnp.where(at == ids_ref[4] * 8 + row, lines, 0.0), axis=1, keepdims=True)
    for x in range(z_ref.shape[2]):
        for i in range(3):
            acc = local_ref[i, x]
            for a in range(8):
                acc = acc + weights[a : a + 1, :] * z_ref[a, i, x].astype(F32)
            out_ref[i, x] = acc


def call(kernel, out_shape, in_specs, scratch=(), flops=0, moved=0, name=None):
    return pl.pallas_call(
        kernel,
        out_shape=[
            shape if isinstance(shape, jax.ShapeDtypeStruct) else jax.ShapeDtypeStruct(shape, F32) for shape in out_shape
        ],
        in_specs=in_specs,
        out_specs=[VMEM] * len(out_shape),
        scratch_shapes=list(scratch),
        compiler_params=pltpu.CompilerParams(vmem_limit_bytes=24 * 2**20),
        cost_estimate=pl.CostEstimate(flops=flops, bytes_accessed=moved, transcendentals=0),
        name=name,
    )


def body(
    deflation,
    residual,
    stiffness,
    mass,
    stencil,
    local_inverse,
    inverse_factor,
    margin_range,
    neighbor_blocks,
):
    vectors, _, cells_x, cells_y, depth = deflation.shape
    n_narrow, size_z = lax.axis_size("narrow"), lax.axis_size("z")
    count = lax.axis_size(WIDE) * n_narrow
    n_near = n_narrow * size_z
    size_y = lax.axis_size("y")

    rounded = residual.astype(jnp.bfloat16)
    couplings = stencil.transpose(1, 2, 0)
    ids = neighbor_blocks.reshape(-1)
    ranges = margin_range.reshape(-1)

    def swaps(axis):
        size = lax.axis_size(axis)
        even = [(k, k ^ 1) for k in range(size)]
        odd = [(k, ((k + 1) ^ 1) - 1) for k in range(1, size - 1)]
        return even, odd, lax.axis_index(axis) % 2 == 0

    def exchanged(sending_low, sending_high, axis):
        even, odd, is_even = swaps(axis)

        def chosen(first, second):
            return jnp.concatenate([jnp.where(is_even, x, y) for x, y in zip(first, second)], axis=0)

        one = lax.ppermute(chosen(sending_high, sending_low), axis, even)
        two = lax.ppermute(chosen(sending_low, sending_high), axis, odd)
        return one, two, is_even

    vector_fields = deflation.reshape(3 * vectors, cells_x, cells_y, depth)
    fields = (vector_fields, rounded)
    one, two, is_even = exchanged([f[:, 0] for f in fields], [f[:, cells_x - 1] for f in fields], "narrow")

    def matrix(rows):
        return jax.ShapeDtypeStruct((rows, 256), jnp.bfloat16)

    zf, zy, sy, table, own_matrix, x_matrix, y_matrix = call(
        before_kernel,
        [
            (vectors, 3, cells_x, cells_y, depth),
            (2, vectors, 3, 8, depth),
            (2, 8, depth),
            (8, 128),
            matrix(9 * cells_x * cells_y),
            matrix(144),
            matrix(288),
        ],
        [SMEM, SMEM] + [VMEM] * 3,
        [pltpu.VMEM((1, 8, 128), F32)],
        flops=20_000_000,
        moved=1_000_000,
        name="before",
    )(couplings, ids, deflation, rounded, stiffness)
    def joined(rows, partner):
        return jnp.concatenate([rows, lax.ppermute(rows, "z", [(k, partner(k) % size_z) for k in range(size_z)])], axis=0)

    rows_z = joined(inverse_factor, lambda k: k ^ 1)
    one, two, table = lax.optimization_barrier((one, two, table))
    rows_z = joined(rows_z, lambda k: k ^ 2)
    xlo, xhi = jnp.where(is_even, two, one), jnp.where(is_even, one, two)

    def side(y):
        middle = jnp.concatenate([f[:, :, y] for f in fields], axis=0)
        return [jnp.concatenate([xlo[:, y : y + 1], middle, xhi[:, y : y + 1]], axis=1)]

    one, two, is_even = exchanged(side(0), side(cells_y - 1), WIDE)
    ylo, yhi = jnp.where(is_even, two, one), jnp.where(is_even, one, two)

    (table,) = call(
        inner_kernel,
        [(8, 128)],
        [VMEM] * 8,
        [pltpu.VMEM((3 * vectors, 8, 128), F32)],
        flops=10_000_000,
        moved=1_000_000,
        name="inner",
    )(own_matrix, x_matrix, zf, stiffness, mass, xlo, xhi, table)
    rows_z = joined(rows_z, lambda k: k + 2 if k // 2 % 2 else k - 2)
    table, payload = call(
        outer_kernel,
        [(8, 128), (n_near, 1, SLOT * vectors)],
        [VMEM] * 6,
        [pltpu.VMEM((6 * vectors, 8, 128), F32)],
        flops=10_000_000,
        moved=2_000_000,
        name="outer",
    )(y_matrix, table, zy, sy, ylo, yhi)
    got = lax.all_to_all(payload, ("narrow", "z"), 0, 0)
    got = [got] + [lax.ppermute(got, "y", [(k, k ^ step) for k in range(size_y)]) for step in range(1, size_y)]
    got = jnp.stack(got)
    other = lax.ppermute(got, "core", [(0, 1), (1, 0)])
    held = [rows_z, lax.ppermute(rows_z, "core", [(0, 1), (1, 0)])]
    (local,) = call(
        local_kernel,
        [(3, cells_x, cells_y, depth)],
        [SMEM] + [VMEM] * 6,
        [pltpu.VMEM((3, cells_y + 2, 2, 8, depth // 2), F32)] * 2,
        flops=2_000_000,
        moved=3_000_000,
        name="local",
    )(ranges, local_inverse.transpose(0, 1, 3, 2, 4), rounded, xlo, xhi, ylo, yhi)

    group = ("narrow", "y")
    members = lax.axis_size(group)

    def spread(share):
        return lax.all_to_all(share, group, 0, 0)

    steps = jnp.arange(size_y, dtype=jnp.int32) ^ lax.axis_index("y")
    core = jnp.append(steps, lax.axis_index("core").astype(jnp.int32))
    flat = (count * vectors // 128, 128)
    packed, slots, rhs, share = call(
        functools.partial(first_kernel, n_narrow, size_z),
        [
            (SLOT * vectors, count),
            jax.ShapeDtypeStruct((count, count * vectors), jnp.bfloat16),
            flat,
            (members,) + flat,
        ],
        [SMEM] + [VMEM] * 4,
        [pltpu.VMEM((count, SLOT * vectors), F32)],
        flops=2_000_000,
        moved=3_000_000,
        name="first",
    )(core, got, other, *held)
    first, share = call(
        functools.partial(second_kernel, n_narrow),
        [flat, (members,) + flat],
        [VMEM] * 6,
        flops=2_000_000,
        moved=3_000_000,
        name="second",
    )(packed, slots, rhs, spread(share), *held)
    preconditioned, solved = call(
        last_kernel,
        [(3, cells_x, cells_y, depth), flat],
        [SMEM] + [VMEM] * 4,
        flops=1_000_000,
        moved=1_000_000,
        name="last",
    )(ids, deflation, local, first, spread(share))
    coarse_solution = solved.reshape(-1)
    blocks = table[:, : 9 * vectors].reshape(vectors, 9, vectors).transpose(1, 0, 2)
    return preconditioned, blocks.reshape(1, 1, 9, vectors, vectors), coarse_solution


def solution(mesh):
    n_narrow, n_wide = mesh.devices.shape
    fine = jax.sharding.Mesh(mesh.devices.reshape(n_narrow, n_wide // 16, 8, 2), ("narrow",) + WIDE)
    placed = (
        P(None, None, "narrow", WIDE, None),
        P(None, "narrow", WIDE, None),
        P("narrow", WIDE, None),
        P("narrow", WIDE, None),
        P(),
        P(None, None, "narrow", WIDE, None),
        P(("narrow",) + WIDE, None),
        P("narrow", WIDE, None, None),
        P("narrow", WIDE, None),
    )
    return jax.shard_map(
        body,
        mesh=fine,
        in_specs=placed,
        out_specs=(P(None, "narrow", WIDE, None), P("narrow", WIDE, None, None, None), P()),
        check_vma=False,
    )
```

```python
import functools

import jax
import jax.numpy as jnp
from jax import lax
from jax.experimental import pallas as pl
from jax.experimental.pallas import tpu as pltpu
from jax.sharding import PartitionSpec as P

F32 = jnp.float32
WIDE = ("y", "z", "core")
SLOT = 80
VMEM = pl.BlockSpec(memory_space=pltpu.VMEM)
SMEM = pl.BlockSpec(memory_space=pltpu.SMEM)


def shifted(value, offset, axis):
    if offset == 0:
        return value
    size = value.shape[axis]
    rolled = pltpu.roll(value, (-offset) % size, axis)
    at = lax.broadcasted_iota(jnp.int32, value.shape, axis)
    keep = at < size - offset if offset > 0 else at >= -offset
    return jnp.where(keep, rolled, 0.0)


def rows_sum(value):
    return jnp.sum(value[:, :128] + value[:, 128:], axis=0, keepdims=True)


def entry(s_ref, ox, oy, oz, i, j):
    return s_ref[i, j, ((ox + 1) * 3 + oy + 1) * 3 + oz + 1]


def faces(total):
    return jnp.sum(total, axis=1, keepdims=True)


def halved(value):
    high = value.astype(jnp.bfloat16)
    return high, (value - high.astype(F32)).astype(jnp.bfloat16)


def laid(s_ref, out_ref, begin, rows, choices):
    value = jnp.zeros((rows, 128), F32)
    for mask, which in choices:
        value = jnp.where(mask, entry(s_ref, *which), value)
    high, low = halved(value)
    out_ref[begin : begin + rows, :128] = high
    out_ref[begin : begin + rows, 128:] = low


def matrices(s_ref, own_ref, x_ref, y_ref, cells_x, cells_y):
    rows = cells_x * cells_y
    row = lax.broadcasted_iota(jnp.int32, (rows, 128), 0)
    col = lax.broadcasted_iota(jnp.int32, (rows, 128), 1)
    dx = col // cells_y % cells_x - row // cells_y
    dy = col % cells_y - row % cells_y
    masks = []
    for j in range(3):
        for ox in (-1, 0, 1):
            for oy in (-1, 0, 1):
                masks.append((j, ox, oy, (col // rows == j) & (dx == ox) & (dy == oy)))
    for oz in (-1, 0, 1):
        for i in range(3):
            choices = [(mask, (ox, oy, oz, i, j)) for j, ox, oy, mask in masks]
            laid(s_ref, own_ref, ((oz + 1) * 3 + i) * rows, rows, choices)
    row = lax.broadcasted_iota(jnp.int32, (8, 128), 0)
    col = lax.broadcasted_iota(jnp.int32, (8, 128), 1)
    at = col % 8
    for oz in (-1, 0, 1):
        for face in range(2):
            side = 2 * face - 1
            here = [col // 8 == face * 3 + j for j in range(3)]
            for i in range(3):
                choices = [
                    (here[j] & (at - row == oy), (side, oy, oz, i, j)) for j in range(3) for oy in (-1, 0, 1)
                ]
                laid(s_ref, x_ref, (((oz + 1) * 2 + face) * 3 + i) * 8, 8, choices)
                inside = (row < cells_x) & (at >= 1) & (at <= cells_x)
                choices = [
                    (here[j] & inside & (at - 1 - row == ox), (ox, side, oz, i, j))
                    for j in range(3)
                    for ox in (-1, 0, 1)
                ]
                laid(s_ref, y_ref, ((((oz + 1) * 2 + face) * 2) * 3 + i) * 8, 8, choices)
                choices = []
                for j in range(3):
                    choices.append((here[j] & (row == 0) & (at == 0), (-1, side, oz, i, j)))
                    choices.append((here[j] & (row == cells_x - 1) & (at == cells_x + 1), (1, side, oz, i, j)))
                laid(s_ref, y_ref, ((((oz + 1) * 2 + face) * 2 + 1) * 3 + i) * 8, 8, choices)


def images(matrix, cells):
    blank = jnp.zeros((128 - cells.shape[0], cells.shape[1]), F32)
    twice = jnp.concatenate([cells, blank, cells, blank], axis=0).astype(jnp.bfloat16)
    result = jnp.dot(matrix, twice, preferred_element_type=F32)
    third = result.shape[0] // 3
    low, mid, high = result[:third], result[third : 2 * third], result[2 * third :]
    return shifted(low, -1, 1) + mid + shifted(high, 1, 1)


def before_kernel(
    s_ref, ids_ref, z_ref, r_ref, stiff_ref, zf_ref, zy_ref, sy_ref, table_ref, own_ref, x_ref, y_ref, rows_ref
):
    vectors, _, cells_x, cells_y, depth = z_ref.shape
    own_y = (0, cells_y - 1)
    blank = jnp.zeros((8 - cells_x, depth), F32)

    def columns(rows):
        return jnp.concatenate(rows + [blank], axis=0)

    matrices(s_ref, own_ref, x_ref, y_ref, cells_x, cells_y)

    def convert(a, carry):
        for i in range(3):
            cells = [z_ref[a, i, x].astype(F32) for x in range(cells_x)]
            for x in range(cells_x):
                zf_ref[a, i, x] = cells[x]
            for face, y in enumerate(own_y):
                zy_ref[face, a, i] = columns([cell[y : y + 1, :] for cell in cells])
        return carry

    lax.fori_loop(0, vectors, convert, 0)
    for face, y in enumerate(own_y):
        sy_ref[face] = columns([stiff_ref[x, y : y + 1, :] for x in range(cells_x)])
    for a in range(vectors):
        total = None
        for i in range(3):
            for x in range(cells_x):
                term = zf_ref[a, i, x] * r_ref[i, x].astype(F32)
                total = term if total is None else total + term
        rows_ref[0, a : a + 1, :] = rows_sum(total)

    lane = lax.broadcasted_iota(jnp.int32, (8, 128), 1)
    table = jnp.where(lane == 9 * vectors + 1, ids_ref[4].astype(F32), 0.0)
    table_ref[...] = jnp.where(lane == 9 * vectors, faces(rows_ref[0]), table)


def inner_kernel(
    own_ref, x_ref, zf_ref, stiff_ref, mass_ref, xlo_ref, xhi_ref, before_ref, table_ref, rows_ref
):
    vectors, _, cells_x, cells_y, depth = zf_ref.shape
    own_x = (0, cells_x - 1)

    def one(b, carry):
        cells = zf_ref[b].reshape(3 * cells_x * cells_y, depth)
        image = images(own_ref[...], cells).reshape(3, cells_x, cells_y, depth)
        weighted = [
            [stiff_ref[x] * image[i, x] + mass_ref[x] * zf_ref[b, i, x] for x in range(cells_x)] for i in range(3)
        ]
        for a in range(vectors):
            total = None
            for i in range(3):
                for x in range(cells_x):
                    term = zf_ref[a, i, x] * weighted[i][x]
                    total = term if total is None else total + term
            rows_ref[vectors + b, a : a + 1, :] = rows_sum(total)
        cells = [halo_ref[b * 3 + j].astype(F32) for halo_ref in (xlo_ref, xhi_ref) for j in range(3)]
        image = images(x_ref[...], jnp.concatenate(cells, axis=0))
        for face in range(2):
            stiff = stiff_ref[own_x[face]]
            weighted = [stiff * image[(face * 3 + i) * 8 : (face * 3 + i + 1) * 8] for i in range(3)]
            for a in range(vectors):
                total = sum(zf_ref[a, i, own_x[face]] * weighted[i] for i in range(3))
                rows_ref[2 * face * vectors + b, a : a + 1, :] = rows_sum(total)
        return carry

    lax.fori_loop(0, vectors, one, 0, unroll=4)
    lane = lax.broadcasted_iota(jnp.int32, (8, 128), 1)
    table = before_ref[...]
    for place, number in enumerate((1, 4, 7)):
        for b in range(vectors):
            table = jnp.where(lane == number * vectors + b, faces(rows_ref[place * vectors + b]), table)
    table_ref[...] = table


def outer_kernel(y_ref, table_ref, zy_ref, sy_ref, ylo_ref, yhi_ref, blocks_ref, pay_ref, rows_ref):
    vectors, depth = zy_ref.shape[1], zy_ref.shape[4]
    cells_x = ylo_ref.shape[1] - 2
    pad = jnp.zeros((8 - ylo_ref.shape[1], depth), F32)

    def one(b, carry):
        cells = []
        for halo_ref in (ylo_ref, yhi_ref):
            for j in range(3):
                cells += [halo_ref[b * 3 + j].astype(F32), pad]
        image = images(y_ref[...], jnp.concatenate(cells, axis=0))
        for face in range(2):
            stiff = sy_ref[face]
            begin = face * 6
            inner = [stiff * image[(begin + i) * 8 : (begin + i + 1) * 8] for i in range(3)]
            outer = [stiff * image[(begin + 3 + i) * 8 : (begin + 4 + i) * 8] for i in range(3)]
            for a in range(vectors):
                own = [zy_ref[face, a, i] for i in range(3)]
                total = sum(own[i] * inner[i] for i in range(3))
                rows_ref[(3 * face + 1) * vectors + b, a : a + 1, :] = rows_sum(total)
                total = sum(own[i] * outer[i] for i in range(3))
                half = total[:, :128] + total[:, 128:]
                rows_ref[3 * face * vectors + b, a : a + 1, :] = half[0:1, :]
                rows_ref[(3 * face + 2) * vectors + b, a : a + 1, :] = half[cells_x - 1 : cells_x, :]
        return carry

    lax.fori_loop(0, vectors, one, 0, unroll=8)
    lane = lax.broadcasted_iota(jnp.int32, (8, 128), 1)
    table = table_ref[...]
    for place, number in enumerate((0, 3, 6, 2, 5, 8)):
        for b in range(vectors):
            table = jnp.where(lane == number * vectors + b, faces(rows_ref[place * vectors + b]), table)
    blocks_ref[...] = table
    width = pay_ref.shape[2]
    wide = jnp.concatenate([table, jnp.zeros((8, width - 128), F32)], axis=1)
    line = jnp.zeros((1, width), F32)
    for a in range(vectors):
        piece = wide[a : a + 1, :]
        line = line + (pltpu.roll(piece, a * SLOT, 1) if a else piece)
    for place in range(pay_ref.shape[0]):
        pay_ref[place] = line


def local_kernel(
    range_ref, inverse_ref, r_ref, xlo_ref, xhi_ref, ylo_ref, yhi_ref, table_ref, out_ref, blocks_ref, ext_ref, sol_ref
):
    table = table_ref[...]
    lane = lax.broadcasted_iota(jnp.int32, table.shape, 1)
    for b in range(8):
        lines = jnp.zeros(table.shape, F32)
        for n in range(9):
            lines = jnp.where(lane == n, table[:, n * 8 + b : n * 8 + b + 1], lines)
        blocks_ref[:, b, :] = lines[:, :9]
    cells_x, cells_y = r_ref.shape[1:3]
    ext_x, ext_y = cells_x + 2, cells_y + 2
    half_x, half_y = ext_x // 2, ext_y // 2
    first = xlo_ref.shape[0] - 3
    halves = ((0, slice(0, 128)), (1, slice(128, 256)))
    for c in range(3):
        layers = [xlo_ref[first + c]] + [r_ref[c, x] for x in range(cells_x)] + [xhi_ref[first + c]]
        layers = [layer.astype(F32) for layer in layers]
        low, high = ylo_ref[first + c].astype(F32), yhi_ref[first + c].astype(F32)
        for h, lanes in halves:
            ext_ref[c, 0, h, 0:ext_x, :] = low[:, lanes]
            ext_ref[c, ext_y - 1, h, 0:ext_x, :] = high[:, lanes]
            for e, layer in enumerate(layers):
                for y in range(cells_y):
                    ext_ref[c, y + 1, h, e : e + 1, :] = layer[y : y + 1, lanes]
    at = lax.broadcasted_iota(jnp.int32, (half_x, r_ref.shape[3]), 0)
    for v in range(half_y):
        fields = []
        for m in range(12):
            c, s, t = m // 4, m // 2 % 2, m % 2
            e, f = 2 * at + s, 2 * v + t
            keep = (f >= range_ref[2]) & (f < range_ref[3]) & (e >= range_ref[0]) & (e < range_ref[1])
            value = jnp.concatenate([ext_ref[c, f, h, pl.ds(s, half_x, stride=2), :] for h, _ in halves], axis=1)
            fields.append(jnp.where(keep, value, 0.0))
        for i in range(12):
            acc = None
            for m in range(12):
                term = inverse_ref[i, m, v].astype(F32) * fields[m]
                acc = term if acc is None else acc + term
            c, s, t = i // 4, i // 2 % 2, i % 2
            for h, lanes in halves:
                sol_ref[c, 2 * v + t, h, pl.ds(s, half_x, stride=2), :] = acc[:, lanes]
    for c in range(3):
        for y in range(cells_y):
            for h, lanes in halves:
                for x in range(cells_x):
                    out_ref[c, x, y : y + 1, lanes] = sol_ref[c, y + 1, h, x + 1 : x + 2, :]


def moved_by(value, choice, dims):
    high = value.astype(jnp.bfloat16).astype(F32)
    middle = (value - high).astype(jnp.bfloat16).astype(F32)
    parts = jnp.concatenate([high, middle, (value - high) - middle], axis=0).astype(jnp.bfloat16)
    result = lax.dot_general(parts, choice, (dims, ((), ())), preferred_element_type=F32)
    return (result[0:8] + result[8:16]) + result[16:24]


def lines_of(flat):
    size = flat.shape[0]
    return jnp.concatenate([jnp.broadcast_to(flat[q : q + 1, :], (8, 128)) for q in range(size)], axis=1)


def flat_of(by_vector):
    at = lax.broadcasted_iota(jnp.int32, by_vector.shape, 1)
    row = lax.broadcasted_iota(jnp.int32, by_vector.shape, 0)
    line = jnp.sum(jnp.where(at % 8 == row, by_vector, 0.0), axis=0, keepdims=True)
    return folded(line)


def folded(line):
    return jnp.concatenate([line[:, q * 128 : (q + 1) * 128] for q in range(line.shape[1] // 128)], axis=0)


def share_of(flat, pieces):
    line = lines_of(flat)
    acc = jnp.zeros(line.shape, F32)
    group = 4
    for piece in pieces:

        def step(t, acc, piece=piece):
            tiles, inner = [], []
            for q in range(group):
                tile = piece[pl.ds(pl.multiple_of((t * group + q) * 8, 8), 8), :]
                tiles.append(tile)
                inner.append(jnp.sum(tile * line, axis=1, keepdims=True))
            for tile, value in zip(tiles, inner):
                acc = acc + tile * value
            return acc

        acc = lax.fori_loop(0, piece.shape[0] // 8 // group, step, acc)
    return folded(jnp.sum(acc, axis=0, keepdims=True))


def first_kernel(
    n_narrow, size_z, row_ref, core_ref, own_ref, other_ref, held_ref, held_other_ref, packed_ref, slots_ref, rhs_ref, share_ref, rows_ref
):
    size_y = own_ref.shape[0]
    chips = n_narrow * size_y * size_z
    for got_ref, core in ((own_ref, core_ref[0]), (other_ref, 1 - core_ref[0])):
        for y in range(size_y):
            step = jnp.bitwise_xor(row_ref[0], y)
            for x in range(n_narrow):
                place = pl.multiple_of(core * chips + (x * size_y + y) * size_z, 8)
                block = got_ref[step, x * size_z : (x + 1) * size_z]
                rows_ref[pl.ds(place, size_z), :] = block.reshape(size_z, block.shape[2])
    rows = rows_ref[...]
    ids = jnp.broadcast_to(rows[:, 73:74].astype(jnp.int32), slots_ref.shape)
    at = lax.broadcasted_iota(jnp.int32, slots_ref.shape, 1)
    slots_ref[...] = (at // 8 == ids).astype(F32).astype(jnp.bfloat16)
    packed = rows.T
    packed_ref[...] = packed
    own = jnp.concatenate([packed[a * SLOT + 72 : a * SLOT + 73, :] for a in range(8)], axis=0)
    rhs = flat_of(moved_by(own, slots_ref[...], ((1,), (0,))))
    rhs_ref[...] = rhs
    share = share_of(rhs, (held_ref, held_other_ref))
    for place in range(share_ref.shape[0]):
        share_ref[place] = share


def summed(parts_ref):
    parts = [parts_ref[k] for k in range(parts_ref.shape[0])]
    while len(parts) > 1:
        parts = [parts[k] + parts[k + 1] for k in range(0, len(parts), 2)]
    return parts[0]


def second_kernel(
    n_narrow, packed_ref, slots_ref, rhs_ref, parts_ref, own_ref, other_ref, first_ref, share_ref
):
    first = summed(parts_ref)
    first_ref[...] = first
    lines = lines_of(first)
    at = lax.broadcasted_iota(jnp.int32, lines.shape, 1)
    entry_at = lax.broadcasted_iota(jnp.int32, lines.shape, 0)
    lines = jnp.where(at % 8 == entry_at, lines, 0.0)
    there = moved_by(lines, slots_ref[...], ((1,), (1,)))
    size = there.shape[1] // 2
    chips = size // n_narrow
    halves = [there[:, :size], there[:, size:]]
    at = lax.broadcasted_iota(jnp.int32, halves[0].shape, 1)
    row, column = at // chips, at % chips
    near = []
    for dx in (-1, 0, 1):
        for dy in (-1, 0, 1):
            sides = []
            for core in range(2):
                step = (core + dy) // 2
                move = (-(dx * chips + step)) % size
                value = halves[(core + dy) % 2]
                value = pltpu.roll(value, move, 1) if move else value
                keep = (row + dx >= 0) & (row + dx < n_narrow) & (column + step >= 0) & (column + step < chips)
                sides.append(jnp.where(keep, value, 0.0))
            near.append(jnp.concatenate(sides, axis=1))
    near.append(jnp.zeros_like(there))
    near = jnp.concatenate(near, axis=0)
    image = jnp.concatenate(
        [jnp.sum(packed_ref[a * SLOT : (a + 1) * SLOT, :] * near, axis=0, keepdims=True) for a in range(8)], axis=0
    )
    vector = rhs_ref[...] - flat_of(moved_by(image, slots_ref[...], ((1,), (0,))))
    share = share_of(vector, (own_ref, other_ref))
    for place in range(share_ref.shape[0]):
        share_ref[place] = share


def last_kernel(ids_ref, z_ref, local_ref, first_ref, parts_ref, out_ref, sol_ref):
    solution = first_ref[...] + summed(parts_ref)
    sol_ref[...] = solution
    lines = lines_of(solution)
    at = lax.broadcasted_iota(jnp.int32, lines.shape, 1)
    row = lax.broadcasted_iota(jnp.int32, lines.shape, 0)
    weights = jnp.sum(jnp.where(at == ids_ref[4] * 8 + row, lines, 0.0), axis=1, keepdims=True)
    for x in range(z_ref.shape[2]):
        for i in range(3):
            acc = local_ref[i, x]
            for a in range(8):
                acc = acc + weights[a : a + 1, :] * z_ref[a, i, x].astype(F32)
            out_ref[i, x] = acc


def call(kernel, out_shape, in_specs, scratch=(), flops=0, moved=0, name=None):
    return pl.pallas_call(
        kernel,
        out_shape=[
            shape if isinstance(shape, jax.ShapeDtypeStruct) else jax.ShapeDtypeStruct(shape, F32) for shape in out_shape
        ],
        in_specs=in_specs,
        out_specs=[VMEM] * len(out_shape),
        scratch_shapes=list(scratch),
        compiler_params=pltpu.CompilerParams(vmem_limit_bytes=24 * 2**20),
        cost_estimate=pl.CostEstimate(flops=flops, bytes_accessed=moved, transcendentals=0),
        name=name,
    )


def body(
    deflation,
    residual,
    stiffness,
    mass,
    stencil,
    local_inverse,
    inverse_factor,
    margin_range,
    neighbor_blocks,
):
    vectors, _, cells_x, cells_y, depth = deflation.shape
    n_narrow, size_z = lax.axis_size("narrow"), lax.axis_size("z")
    count = lax.axis_size(WIDE) * n_narrow
    n_near = n_narrow * size_z
    size_y = lax.axis_size("y")

    rounded = residual.astype(jnp.bfloat16)
    couplings = stencil.transpose(1, 2, 0)
    ids = neighbor_blocks.reshape(-1)
    ranges = margin_range.reshape(-1)

    def swaps(axis):
        size = lax.axis_size(axis)
        even = [(k, k ^ 1) for k in range(size)]
        odd = [(k, ((k + 1) ^ 1) - 1) for k in range(1, size - 1)]
        return even, odd, lax.axis_index(axis) % 2 == 0

    def exchanged(sending_low, sending_high, axis):
        even, odd, is_even = swaps(axis)

        def chosen(first, second):
            return jnp.concatenate([jnp.where(is_even, x, y) for x, y in zip(first, second)], axis=0)

        one = lax.ppermute(chosen(sending_high, sending_low), axis, even)
        two = lax.ppermute(chosen(sending_low, sending_high), axis, odd)
        return one, two, is_even

    vector_fields = deflation.reshape(3 * vectors, cells_x, cells_y, depth)
    fields = (vector_fields, rounded)
    one, two, is_even = exchanged([f[:, 0] for f in fields], [f[:, cells_x - 1] for f in fields], "narrow")

    def matrix(rows):
        return jax.ShapeDtypeStruct((rows, 256), jnp.bfloat16)

    zf, zy, sy, table, own_matrix, x_matrix, y_matrix = call(
        before_kernel,
        [
            (vectors, 3, cells_x, cells_y, depth),
            (2, vectors, 3, 8, depth),
            (2, 8, depth),
            (8, 128),
            matrix(9 * cells_x * cells_y),
            matrix(144),
            matrix(288),
        ],
        [SMEM, SMEM] + [VMEM] * 3,
        [pltpu.VMEM((1, 8, 128), F32)],
        flops=20_000_000,
        moved=1_000_000,
        name="before",
    )(couplings, ids, deflation, rounded, stiffness)
    def joined(rows, partner):
        return jnp.concatenate([rows, lax.ppermute(rows, "z", [(k, partner(k) % size_z) for k in range(size_z)])], axis=0)

    rows_z = joined(inverse_factor, lambda k: k ^ 1)
    one, two, table = lax.optimization_barrier((one, two, table))
    rows_z = joined(rows_z, lambda k: k ^ 2)
    xlo, xhi = jnp.where(is_even, two, one), jnp.where(is_even, one, two)

    def side(y):
        middle = jnp.concatenate([f[:, :, y] for f in fields], axis=0)
        return [jnp.concatenate([xlo[:, y : y + 1], middle, xhi[:, y : y + 1]], axis=1)]

    one, two, is_even = exchanged(side(0), side(cells_y - 1), WIDE)
    ylo, yhi = jnp.where(is_even, two, one), jnp.where(is_even, one, two)

    (table,) = call(
        inner_kernel,
        [(8, 128)],
        [VMEM] * 8,
        [pltpu.VMEM((3 * vectors, 8, 128), F32)],
        flops=10_000_000,
        moved=1_000_000,
        name="inner",
    )(own_matrix, x_matrix, zf, stiffness, mass, xlo, xhi, table)
    rows_z = joined(rows_z, lambda k: k + 2 if k // 2 % 2 else k - 2)
    table, payload = call(
        outer_kernel,
        [(8, 128), (n_near, 1, SLOT * vectors)],
        [VMEM] * 6,
        [pltpu.VMEM((6 * vectors, 8, 128), F32)],
        flops=10_000_000,
        moved=2_000_000,
        name="outer",
    )(y_matrix, table, zy, sy, ylo, yhi)
    got = lax.all_to_all(payload, ("narrow", "z"), 0, 0)
    local, blocks = call(
        local_kernel,
        [(3, cells_x, cells_y, depth), (vectors, vectors, 9)],
        [SMEM] + [VMEM] * 7,
        [pltpu.VMEM((3, cells_y + 2, 2, 8, depth // 2), F32)] * 2,
        flops=2_000_000,
        moved=3_000_000,
        name="local",
    )(ranges, local_inverse.transpose(0, 1, 3, 2, 4), rounded, xlo, xhi, ylo, yhi, table)
    got, local = lax.optimization_barrier((got, local))
    got = [got] + [lax.ppermute(got, "y", [(k, k ^ step) for k in range(size_y)]) for step in range(1, size_y)]
    got = jnp.stack(got)
    other = lax.ppermute(got, "core", [(0, 1), (1, 0)])
    held = [rows_z, lax.ppermute(rows_z, "core", [(0, 1), (1, 0)])]
    group = ("narrow", "y")
    members = lax.axis_size(group)

    def spread(share):
        return lax.all_to_all(share, group, 0, 0)

    row = lax.axis_index("y").astype(jnp.int32).reshape(1)
    core = lax.axis_index("core").astype(jnp.int32).reshape(1)
    flat = (count * vectors // 128, 128)
    packed, slots, rhs, share = call(
        functools.partial(first_kernel, n_narrow, size_z),
        [
            (SLOT * vectors, count),
            jax.ShapeDtypeStruct((count, count * vectors), jnp.bfloat16),
            flat,
            (members,) + flat,
        ],
        [SMEM] * 2 + [VMEM] * 4,
        [pltpu.VMEM((count, SLOT * vectors), F32)],
        flops=2_000_000,
        moved=3_000_000,
        name="first",
    )(row, core, got, other, *held)
    first, share = call(
        functools.partial(second_kernel, n_narrow),
        [flat, (members,) + flat],
        [VMEM] * 6,
        flops=2_000_000,
        moved=3_000_000,
        name="second",
    )(packed, slots, rhs, spread(share), *held)
    preconditioned, solved = call(
        last_kernel,
        [(3, cells_x, cells_y, depth), flat],
        [SMEM] + [VMEM] * 4,
        flops=1_000_000,
        moved=1_000_000,
        name="last",
    )(ids, deflation, local, first, spread(share))
    coarse_solution = solved.reshape(-1)
    blocks = blocks.transpose(2, 0, 1)
    return preconditioned, blocks.reshape(1, 1, 9, vectors, vectors), coarse_solution


def solution(mesh):
    n_narrow, n_wide = mesh.devices.shape
    fine = jax.sharding.Mesh(mesh.devices.reshape(n_narrow, n_wide // 16, 8, 2), ("narrow",) + WIDE)
    placed = (
        P(None, None, "narrow", WIDE, None),
        P(None, "narrow", WIDE, None),
        P("narrow", WIDE, None),
        P("narrow", WIDE, None),
        P(),
        P(None, None, "narrow", WIDE, None),
        P(("narrow",) + WIDE, None),
        P("narrow", WIDE, None, None),
        P("narrow", WIDE, None),
    )
    return jax.shard_map(
        body,
        mesh=fine,
        in_specs=placed,
        out_specs=(P(None, "narrow", WIDE, None), P("narrow", WIDE, None, None, None), P()),
        check_vma=False,
    )
```

```python
import functools

import jax
import jax.numpy as jnp
from jax import lax
from jax.experimental import pallas as pl
from jax.experimental.pallas import tpu as pltpu
from jax.sharding import PartitionSpec as P

F32 = jnp.float32
WIDE = ("y", "z", "core")
SLOT = 80
VMEM = pl.BlockSpec(memory_space=pltpu.VMEM)
SMEM = pl.BlockSpec(memory_space=pltpu.SMEM)


def shifted(value, offset, axis):
    if offset == 0:
        return value
    size = value.shape[axis]
    rolled = pltpu.roll(value, (-offset) % size, axis)
    at = lax.broadcasted_iota(jnp.int32, value.shape, axis)
    keep = at < size - offset if offset > 0 else at >= -offset
    return jnp.where(keep, rolled, 0.0)


def rows_sum(value):
    return jnp.sum(value[:, :128] + value[:, 128:], axis=0, keepdims=True)


def entry(s_ref, ox, oy, oz, i, j):
    return s_ref[i, j, ((ox + 1) * 3 + oy + 1) * 3 + oz + 1]


def faces(total):
    return jnp.sum(total, axis=1, keepdims=True)


def halved(value):
    high = value.astype(jnp.bfloat16)
    return high, (value - high.astype(F32)).astype(jnp.bfloat16)


def laid(s_ref, out_ref, begin, rows, choices):
    value = jnp.zeros((rows, 128), F32)
    for mask, which in choices:
        value = jnp.where(mask, entry(s_ref, *which), value)
    high, low = halved(value)
    out_ref[begin : begin + rows, :128] = high
    out_ref[begin : begin + rows, 128:] = low


def matrices(s_ref, own_ref, x_ref, y_ref, cells_x, cells_y):
    rows = cells_x * cells_y
    row = lax.broadcasted_iota(jnp.int32, (rows, 128), 0)
    col = lax.broadcasted_iota(jnp.int32, (rows, 128), 1)
    dx = col // cells_y % cells_x - row // cells_y
    dy = col % cells_y - row % cells_y
    masks = []
    for j in range(3):
        for ox in (-1, 0, 1):
            for oy in (-1, 0, 1):
                masks.append((j, ox, oy, (col // rows == j) & (dx == ox) & (dy == oy)))
    for oz in (-1, 0, 1):
        for i in range(3):
            choices = [(mask, (ox, oy, oz, i, j)) for j, ox, oy, mask in masks]
            laid(s_ref, own_ref, ((oz + 1) * 3 + i) * rows, rows, choices)
    row = lax.broadcasted_iota(jnp.int32, (8, 128), 0)
    col = lax.broadcasted_iota(jnp.int32, (8, 128), 1)
    at = col % 8
    for oz in (-1, 0, 1):
        for face in range(2):
            side = 2 * face - 1
            here = [col // 8 == face * 3 + j for j in range(3)]
            for i in range(3):
                choices = [
                    (here[j] & (at - row == oy), (side, oy, oz, i, j)) for j in range(3) for oy in (-1, 0, 1)
                ]
                laid(s_ref, x_ref, (((oz + 1) * 2 + face) * 3 + i) * 8, 8, choices)
                inside = (row < cells_x) & (at >= 1) & (at <= cells_x)
                choices = [
                    (here[j] & inside & (at - 1 - row == ox), (ox, side, oz, i, j))
                    for j in range(3)
                    for ox in (-1, 0, 1)
                ]
                laid(s_ref, y_ref, ((((oz + 1) * 2 + face) * 2) * 3 + i) * 8, 8, choices)
                choices = []
                for j in range(3):
                    choices.append((here[j] & (row == 0) & (at == 0), (-1, side, oz, i, j)))
                    choices.append((here[j] & (row == cells_x - 1) & (at == cells_x + 1), (1, side, oz, i, j)))
                laid(s_ref, y_ref, ((((oz + 1) * 2 + face) * 2 + 1) * 3 + i) * 8, 8, choices)


def images(matrix, cells):
    blank = jnp.zeros((128 - cells.shape[0], cells.shape[1]), F32)
    twice = jnp.concatenate([cells, blank, cells, blank], axis=0).astype(jnp.bfloat16)
    result = jnp.dot(matrix, twice, preferred_element_type=F32)
    third = result.shape[0] // 3
    low, mid, high = result[:third], result[third : 2 * third], result[2 * third :]
    return shifted(low, -1, 1) + mid + shifted(high, 1, 1)


def before_kernel(
    s_ref, ids_ref, z_ref, r_ref, stiff_ref, zf_ref, zy_ref, sy_ref, table_ref, own_ref, x_ref, y_ref, rows_ref
):
    vectors, _, cells_x, cells_y, depth = z_ref.shape
    own_y = (0, cells_y - 1)
    blank = jnp.zeros((8 - cells_x, depth), F32)

    def columns(rows):
        return jnp.concatenate(rows + [blank], axis=0)

    matrices(s_ref, own_ref, x_ref, y_ref, cells_x, cells_y)

    def convert(a, carry):
        for i in range(3):
            cells = [z_ref[a, i, x].astype(F32) for x in range(cells_x)]
            for x in range(cells_x):
                zf_ref[a, i, x] = cells[x]
            for face, y in enumerate(own_y):
                zy_ref[face, a, i] = columns([cell[y : y + 1, :] for cell in cells])
        return carry

    lax.fori_loop(0, vectors, convert, 0)
    for face, y in enumerate(own_y):
        sy_ref[face] = columns([stiff_ref[x, y : y + 1, :] for x in range(cells_x)])
    for a in range(vectors):
        total = None
        for i in range(3):
            for x in range(cells_x):
                term = zf_ref[a, i, x] * r_ref[i, x].astype(F32)
                total = term if total is None else total + term
        rows_ref[0, a : a + 1, :] = rows_sum(total)

    lane = lax.broadcasted_iota(jnp.int32, (8, 128), 1)
    table = jnp.where(lane == 9 * vectors + 1, ids_ref[4].astype(F32), 0.0)
    table_ref[...] = jnp.where(lane == 9 * vectors, faces(rows_ref[0]), table)


def inner_kernel(
    own_ref, x_ref, zf_ref, stiff_ref, mass_ref, xlo_ref, xhi_ref, before_ref, table_ref, rows_ref
):
    vectors, _, cells_x, cells_y, depth = zf_ref.shape
    own_x = (0, cells_x - 1)

    def one(b, carry):
        cells = zf_ref[b].reshape(3 * cells_x * cells_y, depth)
        image = images(own_ref[...], cells).reshape(3, cells_x, cells_y, depth)
        weighted = [
            [stiff_ref[x] * image[i, x] + mass_ref[x] * zf_ref[b, i, x] for x in range(cells_x)] for i in range(3)
        ]
        for a in range(vectors):
            total = None
            for i in range(3):
                for x in range(cells_x):
                    term = zf_ref[a, i, x] * weighted[i][x]
                    total = term if total is None else total + term
            rows_ref[vectors + b, a : a + 1, :] = rows_sum(total)
        cells = [halo_ref[b * 3 + j].astype(F32) for halo_ref in (xlo_ref, xhi_ref) for j in range(3)]
        image = images(x_ref[...], jnp.concatenate(cells, axis=0))
        for face in range(2):
            stiff = stiff_ref[own_x[face]]
            weighted = [stiff * image[(face * 3 + i) * 8 : (face * 3 + i + 1) * 8] for i in range(3)]
            for a in range(vectors):
                total = sum(zf_ref[a, i, own_x[face]] * weighted[i] for i in range(3))
                rows_ref[2 * face * vectors + b, a : a + 1, :] = rows_sum(total)
        return carry

    lax.fori_loop(0, vectors, one, 0, unroll=4)
    lane = lax.broadcasted_iota(jnp.int32, (8, 128), 1)
    table = before_ref[...]
    for place, number in enumerate((1, 4, 7)):
        for b in range(vectors):
            table = jnp.where(lane == number * vectors + b, faces(rows_ref[place * vectors + b]), table)
    table_ref[...] = table


def outer_kernel(y_ref, table_ref, zy_ref, sy_ref, ylo_ref, yhi_ref, blocks_ref, pay_ref, rows_ref):
    vectors, depth = zy_ref.shape[1], zy_ref.shape[4]
    cells_x = ylo_ref.shape[1] - 2
    pad = jnp.zeros((8 - ylo_ref.shape[1], depth), F32)

    def one(b, carry):
        cells = []
        for halo_ref in (ylo_ref, yhi_ref):
            for j in range(3):
                cells += [halo_ref[b * 3 + j].astype(F32), pad]
        image = images(y_ref[...], jnp.concatenate(cells, axis=0))
        for face in range(2):
            stiff = sy_ref[face]
            begin = face * 6
            inner = [stiff * image[(begin + i) * 8 : (begin + i + 1) * 8] for i in range(3)]
            outer = [stiff * image[(begin + 3 + i) * 8 : (begin + 4 + i) * 8] for i in range(3)]
            for a in range(vectors):
                own = [zy_ref[face, a, i] for i in range(3)]
                total = sum(own[i] * inner[i] for i in range(3))
                rows_ref[(3 * face + 1) * vectors + b, a : a + 1, :] = rows_sum(total)
                total = sum(own[i] * outer[i] for i in range(3))
                half = total[:, :128] + total[:, 128:]
                rows_ref[3 * face * vectors + b, a : a + 1, :] = half[0:1, :]
                rows_ref[(3 * face + 2) * vectors + b, a : a + 1, :] = half[cells_x - 1 : cells_x, :]
        return carry

    lax.fori_loop(0, vectors, one, 0, unroll=8)
    lane = lax.broadcasted_iota(jnp.int32, (8, 128), 1)
    table = table_ref[...]
    for place, number in enumerate((0, 3, 6, 2, 5, 8)):
        for b in range(vectors):
            table = jnp.where(lane == number * vectors + b, faces(rows_ref[place * vectors + b]), table)
    blocks_ref[...] = table
    width = pay_ref.shape[2]
    wide = jnp.concatenate([table, jnp.zeros((8, width - 128), F32)], axis=1)
    line = jnp.zeros((1, width), F32)
    for a in range(vectors):
        piece = wide[a : a + 1, :]
        line = line + (pltpu.roll(piece, a * SLOT, 1) if a else piece)
    for place in range(pay_ref.shape[0]):
        pay_ref[place] = line


def local_kernel(
    range_ref, inverse_ref, r_ref, xlo_ref, xhi_ref, ylo_ref, yhi_ref, table_ref, out_ref, blocks_ref, ext_ref, sol_ref
):
    table = table_ref[...]
    lane = lax.broadcasted_iota(jnp.int32, table.shape, 1)
    for b in range(8):
        lines = jnp.zeros(table.shape, F32)
        for n in range(9):
            lines = jnp.where(lane == n, table[:, n * 8 + b : n * 8 + b + 1], lines)
        blocks_ref[:, b, :] = lines[:, :9]
    cells_x, cells_y = r_ref.shape[1:3]
    ext_x, ext_y = cells_x + 2, cells_y + 2
    half_x, half_y = ext_x // 2, ext_y // 2
    first = xlo_ref.shape[0] - 3
    halves = ((0, slice(0, 128)), (1, slice(128, 256)))
    for c in range(3):
        layers = [xlo_ref[first + c]] + [r_ref[c, x] for x in range(cells_x)] + [xhi_ref[first + c]]
        layers = [layer.astype(F32) for layer in layers]
        low, high = ylo_ref[first + c].astype(F32), yhi_ref[first + c].astype(F32)
        for h, lanes in halves:
            ext_ref[c, 0, h, 0:ext_x, :] = low[:, lanes]
            ext_ref[c, ext_y - 1, h, 0:ext_x, :] = high[:, lanes]
            for e, layer in enumerate(layers):
                for y in range(cells_y):
                    ext_ref[c, y + 1, h, e : e + 1, :] = layer[y : y + 1, lanes]
    at = lax.broadcasted_iota(jnp.int32, (half_x, r_ref.shape[3]), 0)
    for v in range(half_y):
        fields = []
        for m in range(12):
            c, s, t = m // 4, m // 2 % 2, m % 2
            e, f = 2 * at + s, 2 * v + t
            keep = (f >= range_ref[2]) & (f < range_ref[3]) & (e >= range_ref[0]) & (e < range_ref[1])
            value = jnp.concatenate([ext_ref[c, f, h, pl.ds(s, half_x, stride=2), :] for h, _ in halves], axis=1)
            fields.append(jnp.where(keep, value, 0.0))
        for i in range(12):
            acc = None
            for m in range(12):
                term = inverse_ref[i, m, v].astype(F32) * fields[m]
                acc = term if acc is None else acc + term
            c, s, t = i // 4, i // 2 % 2, i % 2
            for h, lanes in halves:
                sol_ref[c, 2 * v + t, h, pl.ds(s, half_x, stride=2), :] = acc[:, lanes]
    for c in range(3):
        for y in range(cells_y):
            for h, lanes in halves:
                for x in range(cells_x):
                    out_ref[c, x, y : y + 1, lanes] = sol_ref[c, y + 1, h, x + 1 : x + 2, :]


def moved_by(value, choice, dims):
    high = value.astype(jnp.bfloat16).astype(F32)
    middle = (value - high).astype(jnp.bfloat16).astype(F32)
    parts = jnp.concatenate([high, middle, (value - high) - middle], axis=0).astype(jnp.bfloat16)
    result = lax.dot_general(parts, choice, (dims, ((), ())), preferred_element_type=F32)
    return (result[0:8] + result[8:16]) + result[16:24]


def lines_of(flat):
    size = flat.shape[0]
    return jnp.concatenate([jnp.broadcast_to(flat[q : q + 1, :], (8, 128)) for q in range(size)], axis=1)


def flat_of(by_vector):
    at = lax.broadcasted_iota(jnp.int32, by_vector.shape, 1)
    row = lax.broadcasted_iota(jnp.int32, by_vector.shape, 0)
    line = jnp.sum(jnp.where(at % 8 == row, by_vector, 0.0), axis=0, keepdims=True)
    return folded(line)


def folded(line):
    return jnp.concatenate([line[:, q * 128 : (q + 1) * 128] for q in range(line.shape[1] // 128)], axis=0)


def share_of(flat, pieces):
    line = lines_of(flat)
    acc = jnp.zeros(line.shape, F32)
    group = 4
    for piece in pieces:

        def step(t, acc, piece=piece):
            tiles, inner = [], []
            for q in range(group):
                tile = piece[pl.ds(pl.multiple_of((t * group + q) * 8, 8), 8), :]
                tiles.append(tile)
                inner.append(jnp.sum(tile * line, axis=1, keepdims=True))
            for tile, value in zip(tiles, inner):
                acc = acc + tile * value
            return acc

        acc = lax.fori_loop(0, piece.shape[0] // 8 // group, step, acc)
    return folded(jnp.sum(acc, axis=0, keepdims=True))


def first_kernel(
    n_narrow, size_z, row_ref, core_ref, own_ref, other_ref, held0_ref, held1_ref, held2_ref,
    packed_ref, slots_ref, rhs_ref, share_ref, rows_ref,
):
    size_y = own_ref.shape[0]
    chips = n_narrow * size_y * size_z
    for got_ref, core in ((own_ref, core_ref[0]), (other_ref, 1 - core_ref[0])):
        for y in range(size_y):
            step = jnp.bitwise_xor(row_ref[0], y)
            for x in range(n_narrow):
                place = pl.multiple_of(core * chips + (x * size_y + y) * size_z, 8)
                block = got_ref[step, x * size_z : (x + 1) * size_z]
                rows_ref[pl.ds(place, size_z), :] = block.reshape(size_z, block.shape[2])
    rows = rows_ref[...]
    ids = jnp.broadcast_to(rows[:, 73:74].astype(jnp.int32), slots_ref.shape)
    at = lax.broadcasted_iota(jnp.int32, slots_ref.shape, 1)
    slots_ref[...] = (at // 8 == ids).astype(F32).astype(jnp.bfloat16)
    packed = rows.T
    packed_ref[...] = packed
    own = jnp.concatenate([packed[a * SLOT + 72 : a * SLOT + 73, :] for a in range(8)], axis=0)
    rhs = flat_of(moved_by(own, slots_ref[...], ((1,), (0,))))
    rhs_ref[...] = rhs
    share = share_of(rhs, (held0_ref, held1_ref, held2_ref))
    for place in range(share_ref.shape[0]):
        share_ref[place] = share


def summed(parts_ref):
    parts = [parts_ref[k] for k in range(parts_ref.shape[0])]
    while len(parts) > 1:
        parts = [parts[k] + parts[k + 1] for k in range(0, len(parts), 2)]
    return parts[0]


def second_kernel(
    n_narrow, packed_ref, slots_ref, rhs_ref, parts_ref, held0_ref, held1_ref, held2_ref, first_ref, share_ref
):
    first = summed(parts_ref)
    first_ref[...] = first
    lines = lines_of(first)
    at = lax.broadcasted_iota(jnp.int32, lines.shape, 1)
    entry_at = lax.broadcasted_iota(jnp.int32, lines.shape, 0)
    lines = jnp.where(at % 8 == entry_at, lines, 0.0)
    there = moved_by(lines, slots_ref[...], ((1,), (1,)))
    size = there.shape[1] // 2
    chips = size // n_narrow
    halves = [there[:, :size], there[:, size:]]
    at = lax.broadcasted_iota(jnp.int32, halves[0].shape, 1)
    row, column = at // chips, at % chips
    near = []
    for dx in (-1, 0, 1):
        for dy in (-1, 0, 1):
            sides = []
            for core in range(2):
                step = (core + dy) // 2
                move = (-(dx * chips + step)) % size
                value = halves[(core + dy) % 2]
                value = pltpu.roll(value, move, 1) if move else value
                keep = (row + dx >= 0) & (row + dx < n_narrow) & (column + step >= 0) & (column + step < chips)
                sides.append(jnp.where(keep, value, 0.0))
            near.append(jnp.concatenate(sides, axis=1))
    near.append(jnp.zeros_like(there))
    near = jnp.concatenate(near, axis=0)
    image = jnp.concatenate(
        [jnp.sum(packed_ref[a * SLOT : (a + 1) * SLOT, :] * near, axis=0, keepdims=True) for a in range(8)], axis=0
    )
    vector = rhs_ref[...] - flat_of(moved_by(image, slots_ref[...], ((1,), (0,))))
    share = share_of(vector, (held0_ref, held1_ref, held2_ref))
    for place in range(share_ref.shape[0]):
        share_ref[place] = share


def last_kernel(ids_ref, z_ref, local_ref, first_ref, parts_ref, out_ref, sol_ref):
    solution = first_ref[...] + summed(parts_ref)
    sol_ref[...] = solution
    lines = lines_of(solution)
    at = lax.broadcasted_iota(jnp.int32, lines.shape, 1)
    row = lax.broadcasted_iota(jnp.int32, lines.shape, 0)
    weights = jnp.sum(jnp.where(at == ids_ref[4] * 8 + row, lines, 0.0), axis=1, keepdims=True)
    for x in range(z_ref.shape[2]):
        for i in range(3):
            acc = local_ref[i, x]
            for a in range(8):
                acc = acc + weights[a : a + 1, :] * z_ref[a, i, x].astype(F32)
            out_ref[i, x] = acc


def call(kernel, out_shape, in_specs, scratch=(), flops=0, moved=0, name=None):
    return pl.pallas_call(
        kernel,
        out_shape=[
            shape if isinstance(shape, jax.ShapeDtypeStruct) else jax.ShapeDtypeStruct(shape, F32) for shape in out_shape
        ],
        in_specs=in_specs,
        out_specs=[VMEM] * len(out_shape),
        scratch_shapes=list(scratch),
        compiler_params=pltpu.CompilerParams(vmem_limit_bytes=24 * 2**20),
        cost_estimate=pl.CostEstimate(flops=flops, bytes_accessed=moved, transcendentals=0),
        name=name,
    )


def body(
    deflation,
    residual,
    stiffness,
    mass,
    stencil,
    local_inverse,
    inverse_factor,
    margin_range,
    neighbor_blocks,
):
    vectors, _, cells_x, cells_y, depth = deflation.shape
    n_narrow, size_z = lax.axis_size("narrow"), lax.axis_size("z")
    count = lax.axis_size(WIDE) * n_narrow
    n_near = n_narrow * size_z
    size_y = lax.axis_size("y")

    rounded = residual.astype(jnp.bfloat16)
    couplings = stencil.transpose(1, 2, 0)
    ids = neighbor_blocks.reshape(-1)
    ranges = margin_range.reshape(-1)

    def swaps(axis):
        size = lax.axis_size(axis)
        even = [(k, k ^ 1) for k in range(size)]
        odd = [(k, ((k + 1) ^ 1) - 1) for k in range(1, size - 1)]
        return even, odd, lax.axis_index(axis) % 2 == 0

    def exchanged(sending_low, sending_high, axis):
        even, odd, is_even = swaps(axis)

        def chosen(first, second):
            return jnp.concatenate([jnp.where(is_even, x, y) for x, y in zip(first, second)], axis=0)

        one = lax.ppermute(chosen(sending_high, sending_low), axis, even)
        two = lax.ppermute(chosen(sending_low, sending_high), axis, odd)
        return one, two, is_even

    vector_fields = deflation.reshape(3 * vectors, cells_x, cells_y, depth)
    fields = (vector_fields, rounded)
    one, two, is_even = exchanged([f[:, 0] for f in fields], [f[:, cells_x - 1] for f in fields], "narrow")

    def matrix(rows):
        return jax.ShapeDtypeStruct((rows, 256), jnp.bfloat16)

    zf, zy, sy, table, own_matrix, x_matrix, y_matrix = call(
        before_kernel,
        [
            (vectors, 3, cells_x, cells_y, depth),
            (2, vectors, 3, 8, depth),
            (2, 8, depth),
            (8, 128),
            matrix(9 * cells_x * cells_y),
            matrix(144),
            matrix(288),
        ],
        [SMEM, SMEM] + [VMEM] * 3,
        [pltpu.VMEM((1, 8, 128), F32)],
        flops=20_000_000,
        moved=1_000_000,
        name="before",
    )(couplings, ids, deflation, rounded, stiffness)
    def joined(rows, partner):
        return jnp.concatenate([rows, lax.ppermute(rows, "z", [(k, partner(k) % size_z) for k in range(size_z)])], axis=0)

    rows_z = joined(inverse_factor, lambda k: k ^ 1)
    one, two, table = lax.optimization_barrier((one, two, table))
    rows_z = joined(rows_z, lambda k: k ^ 2)
    xlo, xhi = jnp.where(is_even, two, one), jnp.where(is_even, one, two)

    def side(y):
        middle = jnp.concatenate([f[:, :, y] for f in fields], axis=0)
        return [jnp.concatenate([xlo[:, y : y + 1], middle, xhi[:, y : y + 1]], axis=1)]

    one, two, is_even = exchanged(side(0), side(cells_y - 1), WIDE)
    ylo, yhi = jnp.where(is_even, two, one), jnp.where(is_even, one, two)

    (table,) = call(
        inner_kernel,
        [(8, 128)],
        [VMEM] * 8,
        [pltpu.VMEM((3 * vectors, 8, 128), F32)],
        flops=10_000_000,
        moved=1_000_000,
        name="inner",
    )(own_matrix, x_matrix, zf, stiffness, mass, xlo, xhi, table)
    far_z = lax.ppermute(rows_z, "z", [(k, (k + 2 if k // 2 % 2 else k - 2) % size_z) for k in range(size_z)])
    all_z = jnp.concatenate([rows_z, far_z], axis=0)
    table, payload = call(
        outer_kernel,
        [(8, 128), (n_near, 1, SLOT * vectors)],
        [VMEM] * 6,
        [pltpu.VMEM((6 * vectors, 8, 128), F32)],
        flops=10_000_000,
        moved=2_000_000,
        name="outer",
    )(y_matrix, table, zy, sy, ylo, yhi)
    got = lax.all_to_all(payload, ("narrow", "z"), 0, 0)
    local, blocks = call(
        local_kernel,
        [(3, cells_x, cells_y, depth), (vectors, vectors, 9)],
        [SMEM] + [VMEM] * 7,
        [pltpu.VMEM((3, cells_y + 2, 2, 8, depth // 2), F32)] * 2,
        flops=2_000_000,
        moved=3_000_000,
        name="local",
    )(ranges, local_inverse.transpose(0, 1, 3, 2, 4), rounded, xlo, xhi, ylo, yhi, table)
    got, local = lax.optimization_barrier((got, local))
    got = [got] + [lax.ppermute(got, "y", [(k, k ^ step) for k in range(size_y)]) for step in range(1, size_y)]
    got = jnp.stack(got)
    other = lax.ppermute(got, "core", [(0, 1), (1, 0)])
    held = [rows_z, far_z, lax.ppermute(all_z, "core", [(0, 1), (1, 0)])]
    group = ("narrow", "y")
    members = lax.axis_size(group)

    def spread(share):
        return lax.all_to_all(share, group, 0, 0)

    row = lax.axis_index("y").astype(jnp.int32).reshape(1)
    core = lax.axis_index("core").astype(jnp.int32).reshape(1)
    flat = (count * vectors // 128, 128)
    packed, slots, rhs, share = call(
        functools.partial(first_kernel, n_narrow, size_z),
        [
            (SLOT * vectors, count),
            jax.ShapeDtypeStruct((count, count * vectors), jnp.bfloat16),
            flat,
            (members,) + flat,
        ],
        [SMEM] * 2 + [VMEM] * 5,
        [pltpu.VMEM((count, SLOT * vectors), F32)],
        flops=2_000_000,
        moved=3_000_000,
        name="first",
    )(row, core, got, other, *held)
    first, share = call(
        functools.partial(second_kernel, n_narrow),
        [flat, (members,) + flat],
        [VMEM] * 7,
        flops=2_000_000,
        moved=3_000_000,
        name="second",
    )(packed, slots, rhs, spread(share), *held)
    preconditioned, solved = call(
        last_kernel,
        [(3, cells_x, cells_y, depth), flat],
        [SMEM] + [VMEM] * 4,
        flops=1_000_000,
        moved=1_000_000,
        name="last",
    )(ids, deflation, local, first, spread(share))
    coarse_solution = solved.reshape(-1)
    blocks = blocks.transpose(2, 0, 1)
    return preconditioned, blocks.reshape(1, 1, 9, vectors, vectors), coarse_solution


def solution(mesh):
    n_narrow, n_wide = mesh.devices.shape
    fine = jax.sharding.Mesh(mesh.devices.reshape(n_narrow, n_wide // 16, 8, 2), ("narrow",) + WIDE)
    placed = (
        P(None, None, "narrow", WIDE, None),
        P(None, "narrow", WIDE, None),
        P("narrow", WIDE, None),
        P("narrow", WIDE, None),
        P(),
        P(None, None, "narrow", WIDE, None),
        P(("narrow",) + WIDE, None),
        P("narrow", WIDE, None, None),
        P("narrow", WIDE, None),
    )
    return jax.shard_map(
        body,
        mesh=fine,
        in_specs=placed,
        out_specs=(P(None, "narrow", WIDE, None), P("narrow", WIDE, None, None, None), P()),
        check_vma=False,
    )
```

```python
import functools

import jax
import jax.numpy as jnp
from jax import lax
from jax.experimental import pallas as pl
from jax.experimental.pallas import tpu as pltpu
from jax.sharding import PartitionSpec as P

F32 = jnp.float32
WIDE = ("y", "z", "core")
SLOT = 80
VMEM = pl.BlockSpec(memory_space=pltpu.VMEM)
SMEM = pl.BlockSpec(memory_space=pltpu.SMEM)


def shifted(value, offset, axis):
    if offset == 0:
        return value
    size = value.shape[axis]
    rolled = pltpu.roll(value, (-offset) % size, axis)
    at = lax.broadcasted_iota(jnp.int32, value.shape, axis)
    keep = at < size - offset if offset > 0 else at >= -offset
    return jnp.where(keep, rolled, 0.0)


def rows_sum(value):
    return jnp.sum(value[:, :128] + value[:, 128:], axis=0, keepdims=True)


def entry(s_ref, ox, oy, oz, i, j):
    return s_ref[i, j, ((ox + 1) * 3 + oy + 1) * 3 + oz + 1]


def faces(total):
    return jnp.sum(total, axis=1, keepdims=True)


def halved(value):
    high = value.astype(jnp.bfloat16)
    return high, (value - high.astype(F32)).astype(jnp.bfloat16)


def laid(s_ref, out_ref, begin, rows, choices):
    value = jnp.zeros((rows, 128), F32)
    for mask, which in choices:
        value = jnp.where(mask, entry(s_ref, *which), value)
    high, low = halved(value)
    out_ref[begin : begin + rows, :128] = high
    out_ref[begin : begin + rows, 128:] = low


def matrices(s_ref, own_ref, x_ref, y_ref, cells_x, cells_y):
    rows = cells_x * cells_y
    row = lax.broadcasted_iota(jnp.int32, (rows, 128), 0)
    col = lax.broadcasted_iota(jnp.int32, (rows, 128), 1)
    dx = col // cells_y % cells_x - row // cells_y
    dy = col % cells_y - row % cells_y
    masks = []
    for j in range(3):
        for ox in (-1, 0, 1):
            for oy in (-1, 0, 1):
                masks.append((j, ox, oy, (col // rows == j) & (dx == ox) & (dy == oy)))
    for oz in (-1, 0, 1):
        for i in range(3):
            choices = [(mask, (ox, oy, oz, i, j)) for j, ox, oy, mask in masks]
            laid(s_ref, own_ref, ((oz + 1) * 3 + i) * rows, rows, choices)
    row = lax.broadcasted_iota(jnp.int32, (8, 128), 0)
    col = lax.broadcasted_iota(jnp.int32, (8, 128), 1)
    at = col % 8
    for oz in (-1, 0, 1):
        for face in range(2):
            side = 2 * face - 1
            here = [col // 8 == face * 3 + j for j in range(3)]
            for i in range(3):
                choices = [
                    (here[j] & (at - row == oy), (side, oy, oz, i, j)) for j in range(3) for oy in (-1, 0, 1)
                ]
                laid(s_ref, x_ref, (((oz + 1) * 2 + face) * 3 + i) * 8, 8, choices)
                inside = (row < cells_x) & (at >= 1) & (at <= cells_x)
                choices = [
                    (here[j] & inside & (at - 1 - row == ox), (ox, side, oz, i, j))
                    for j in range(3)
                    for ox in (-1, 0, 1)
                ]
                laid(s_ref, y_ref, ((((oz + 1) * 2 + face) * 2) * 3 + i) * 8, 8, choices)
                choices = []
                for j in range(3):
                    choices.append((here[j] & (row == 0) & (at == 0), (-1, side, oz, i, j)))
                    choices.append((here[j] & (row == cells_x - 1) & (at == cells_x + 1), (1, side, oz, i, j)))
                laid(s_ref, y_ref, ((((oz + 1) * 2 + face) * 2 + 1) * 3 + i) * 8, 8, choices)


def images(matrix, cells):
    blank = jnp.zeros((128 - cells.shape[0], cells.shape[1]), F32)
    twice = jnp.concatenate([cells, blank, cells, blank], axis=0).astype(jnp.bfloat16)
    result = jnp.dot(matrix, twice, preferred_element_type=F32)
    third = result.shape[0] // 3
    low, mid, high = result[:third], result[third : 2 * third], result[2 * third :]
    return shifted(low, -1, 1) + mid + shifted(high, 1, 1)


def before_kernel(
    s_ref, ids_ref, z_ref, r_ref, stiff_ref, zf_ref, zy_ref, sy_ref, table_ref, own_ref, x_ref, y_ref, rows_ref
):
    vectors, _, cells_x, cells_y, depth = z_ref.shape
    own_y = (0, cells_y - 1)
    blank = jnp.zeros((8 - cells_x, depth), F32)

    def columns(rows):
        return jnp.concatenate(rows + [blank], axis=0)

    matrices(s_ref, own_ref, x_ref, y_ref, cells_x, cells_y)

    def convert(a, carry):
        for i in range(3):
            cells = [z_ref[a, i, x].astype(F32) for x in range(cells_x)]
            for x in range(cells_x):
                zf_ref[a, i, x] = cells[x]
            for face, y in enumerate(own_y):
                zy_ref[face, a, i] = columns([cell[y : y + 1, :] for cell in cells])
        return carry

    lax.fori_loop(0, vectors, convert, 0)
    for face, y in enumerate(own_y):
        sy_ref[face] = columns([stiff_ref[x, y : y + 1, :] for x in range(cells_x)])
    for a in range(vectors):
        total = None
        for i in range(3):
            for x in range(cells_x):
                term = zf_ref[a, i, x] * r_ref[i, x].astype(F32)
                total = term if total is None else total + term
        rows_ref[0, a : a + 1, :] = rows_sum(total)

    lane = lax.broadcasted_iota(jnp.int32, (8, 128), 1)
    table = jnp.where(lane == 9 * vectors + 1, ids_ref[4].astype(F32), 0.0)
    table_ref[...] = jnp.where(lane == 9 * vectors, faces(rows_ref[0]), table)


def inner_kernel(
    own_ref, x_ref, zf_ref, stiff_ref, mass_ref, xlo_ref, xhi_ref, before_ref, table_ref, rows_ref
):
    vectors, _, cells_x, cells_y, depth = zf_ref.shape
    own_x = (0, cells_x - 1)

    def one(b, carry):
        cells = zf_ref[b].reshape(3 * cells_x * cells_y, depth)
        image = images(own_ref[...], cells).reshape(3, cells_x, cells_y, depth)
        weighted = [
            [stiff_ref[x] * image[i, x] + mass_ref[x] * zf_ref[b, i, x] for x in range(cells_x)] for i in range(3)
        ]
        for a in range(vectors):
            total = None
            for i in range(3):
                for x in range(cells_x):
                    term = zf_ref[a, i, x] * weighted[i][x]
                    total = term if total is None else total + term
            rows_ref[vectors + b, a : a + 1, :] = rows_sum(total)
        cells = [halo_ref[b * 3 + j].astype(F32) for halo_ref in (xlo_ref, xhi_ref) for j in range(3)]
        image = images(x_ref[...], jnp.concatenate(cells, axis=0))
        for face in range(2):
            stiff = stiff_ref[own_x[face]]
            weighted = [stiff * image[(face * 3 + i) * 8 : (face * 3 + i + 1) * 8] for i in range(3)]
            for a in range(vectors):
                total = sum(zf_ref[a, i, own_x[face]] * weighted[i] for i in range(3))
                rows_ref[2 * face * vectors + b, a : a + 1, :] = rows_sum(total)
        return carry

    lax.fori_loop(0, vectors, one, 0, unroll=4)
    lane = lax.broadcasted_iota(jnp.int32, (8, 128), 1)
    table = before_ref[...]
    for place, number in enumerate((1, 4, 7)):
        for b in range(vectors):
            table = jnp.where(lane == number * vectors + b, faces(rows_ref[place * vectors + b]), table)
    table_ref[...] = table


def outer_kernel(y_ref, table_ref, zy_ref, sy_ref, ylo_ref, yhi_ref, blocks_ref, pay_ref, rows_ref):
    vectors, depth = zy_ref.shape[1], zy_ref.shape[4]
    cells_x = ylo_ref.shape[1] - 2
    pad = jnp.zeros((8 - ylo_ref.shape[1], depth), F32)

    def one(b, carry):
        cells = []
        for halo_ref in (ylo_ref, yhi_ref):
            for j in range(3):
                cells += [halo_ref[b * 3 + j].astype(F32), pad]
        image = images(y_ref[...], jnp.concatenate(cells, axis=0))
        for face in range(2):
            stiff = sy_ref[face]
            begin = face * 6
            inner = [stiff * image[(begin + i) * 8 : (begin + i + 1) * 8] for i in range(3)]
            outer = [stiff * image[(begin + 3 + i) * 8 : (begin + 4 + i) * 8] for i in range(3)]
            for a in range(vectors):
                own = [zy_ref[face, a, i] for i in range(3)]
                total = sum(own[i] * inner[i] for i in range(3))
                rows_ref[(3 * face + 1) * vectors + b, a : a + 1, :] = rows_sum(total)
                total = sum(own[i] * outer[i] for i in range(3))
                half = total[:, :128] + total[:, 128:]
                rows_ref[3 * face * vectors + b, a : a + 1, :] = half[0:1, :]
                rows_ref[(3 * face + 2) * vectors + b, a : a + 1, :] = half[cells_x - 1 : cells_x, :]
        return carry

    lax.fori_loop(0, vectors, one, 0, unroll=8)
    lane = lax.broadcasted_iota(jnp.int32, (8, 128), 1)
    table = table_ref[...]
    for place, number in enumerate((0, 3, 6, 2, 5, 8)):
        for b in range(vectors):
            table = jnp.where(lane == number * vectors + b, faces(rows_ref[place * vectors + b]), table)
    blocks_ref[...] = table
    width = pay_ref.shape[2]
    wide = jnp.concatenate([table, jnp.zeros((8, width - 128), F32)], axis=1)
    line = jnp.zeros((1, width), F32)
    for a in range(vectors):
        piece = wide[a : a + 1, :]
        line = line + (pltpu.roll(piece, a * SLOT, 1) if a else piece)
    for place in range(pay_ref.shape[0]):
        pay_ref[place] = line


def local_kernel(
    range_ref, inverse_ref, r_ref, xlo_ref, xhi_ref, ylo_ref, yhi_ref, table_ref, out_ref, blocks_ref, ext_ref, sol_ref
):
    table = table_ref[...]
    lane = lax.broadcasted_iota(jnp.int32, table.shape, 1)
    for b in range(8):
        lines = jnp.zeros(table.shape, F32)
        for n in range(9):
            lines = jnp.where(lane == n, table[:, n * 8 + b : n * 8 + b + 1], lines)
        blocks_ref[:, b, :] = lines[:, :9]
    cells_x, cells_y = r_ref.shape[1:3]
    ext_x, ext_y = cells_x + 2, cells_y + 2
    half_x, half_y = ext_x // 2, ext_y // 2
    first = xlo_ref.shape[0] - 3
    halves = ((0, slice(0, 128)), (1, slice(128, 256)))
    for c in range(3):
        layers = [xlo_ref[first + c]] + [r_ref[c, x] for x in range(cells_x)] + [xhi_ref[first + c]]
        layers = [layer.astype(F32) for layer in layers]
        low, high = ylo_ref[first + c].astype(F32), yhi_ref[first + c].astype(F32)
        for h, lanes in halves:
            ext_ref[c, 0, h, 0:ext_x, :] = low[:, lanes]
            ext_ref[c, ext_y - 1, h, 0:ext_x, :] = high[:, lanes]
            for e, layer in enumerate(layers):
                for y in range(cells_y):
                    ext_ref[c, y + 1, h, e : e + 1, :] = layer[y : y + 1, lanes]
    at = lax.broadcasted_iota(jnp.int32, (half_x, r_ref.shape[3]), 0)
    for v in range(half_y):
        fields = []
        for m in range(12):
            c, s, t = m // 4, m // 2 % 2, m % 2
            e, f = 2 * at + s, 2 * v + t
            keep = (f >= range_ref[2]) & (f < range_ref[3]) & (e >= range_ref[0]) & (e < range_ref[1])
            value = jnp.concatenate([ext_ref[c, f, h, pl.ds(s, half_x, stride=2), :] for h, _ in halves], axis=1)
            fields.append(jnp.where(keep, value, 0.0))
        for i in range(12):
            acc = None
            for m in range(12):
                term = inverse_ref[i, m, v].astype(F32) * fields[m]
                acc = term if acc is None else acc + term
            c, s, t = i // 4, i // 2 % 2, i % 2
            for h, lanes in halves:
                sol_ref[c, 2 * v + t, h, pl.ds(s, half_x, stride=2), :] = acc[:, lanes]
    for c in range(3):
        for y in range(cells_y):
            for h, lanes in halves:
                for x in range(cells_x):
                    out_ref[c, x, y : y + 1, lanes] = sol_ref[c, y + 1, h, x + 1 : x + 2, :]


def moved_by(value, choice, dims):
    high = value.astype(jnp.bfloat16).astype(F32)
    middle = (value - high).astype(jnp.bfloat16).astype(F32)
    parts = jnp.concatenate([high, middle, (value - high) - middle], axis=0).astype(jnp.bfloat16)
    result = lax.dot_general(parts, choice, (dims, ((), ())), preferred_element_type=F32)
    return (result[0:8] + result[8:16]) + result[16:24]


def lines_of(flat):
    size = flat.shape[0]
    return jnp.concatenate([jnp.broadcast_to(flat[q : q + 1, :], (8, 128)) for q in range(size)], axis=1)


def flat_of(by_vector):
    at = lax.broadcasted_iota(jnp.int32, by_vector.shape, 1)
    row = lax.broadcasted_iota(jnp.int32, by_vector.shape, 0)
    line = jnp.sum(jnp.where(at % 8 == row, by_vector, 0.0), axis=0, keepdims=True)
    return folded(line)


def folded(line):
    return jnp.concatenate([line[:, q * 128 : (q + 1) * 128] for q in range(line.shape[1] // 128)], axis=0)


def share_of(flat, pieces):
    line = lines_of(flat)
    acc = jnp.zeros(line.shape, F32)
    group = 4
    for piece in pieces:

        def step(t, acc, piece=piece):
            tiles, inner = [], []
            for q in range(group):
                tile = piece[pl.ds(pl.multiple_of((t * group + q) * 8, 8), 8), :]
                tiles.append(tile)
                inner.append(jnp.sum(tile * line, axis=1, keepdims=True))
            for tile, value in zip(tiles, inner):
                acc = acc + tile * value
            return acc

        acc = lax.fori_loop(0, piece.shape[0] // 8 // group, step, acc, unroll=True)
    return folded(jnp.sum(acc, axis=0, keepdims=True))


def first_kernel(
    n_narrow, size_z, row_ref, core_ref, own_ref, other_ref, held0_ref, held1_ref, held2_ref,
    packed_ref, slots_ref, rhs_ref, share_ref, rows_ref,
):
    size_y = own_ref.shape[0]
    chips = n_narrow * size_y * size_z
    for got_ref, core in ((own_ref, core_ref[0]), (other_ref, 1 - core_ref[0])):
        for y in range(size_y):
            step = jnp.bitwise_xor(row_ref[0], y)
            for x in range(n_narrow):
                place = pl.multiple_of(core * chips + (x * size_y + y) * size_z, 8)
                block = got_ref[step, x * size_z : (x + 1) * size_z]
                rows_ref[pl.ds(place, size_z), :] = block.reshape(size_z, block.shape[2])
    rows = rows_ref[...]
    ids = jnp.broadcast_to(rows[:, 73:74].astype(jnp.int32), slots_ref.shape)
    at = lax.broadcasted_iota(jnp.int32, slots_ref.shape, 1)
    slots_ref[...] = (at // 8 == ids).astype(F32).astype(jnp.bfloat16)
    packed = rows.T
    packed_ref[...] = packed
    own = jnp.concatenate([packed[a * SLOT + 72 : a * SLOT + 73, :] for a in range(8)], axis=0)
    rhs = flat_of(moved_by(own, slots_ref[...], ((1,), (0,))))
    rhs_ref[...] = rhs
    share = share_of(rhs, (held0_ref, held1_ref, held2_ref))
    for place in range(share_ref.shape[0]):
        share_ref[place] = share


def summed(parts_ref):
    parts = [parts_ref[k] for k in range(parts_ref.shape[0])]
    while len(parts) > 1:
        parts = [parts[k] + parts[k + 1] for k in range(0, len(parts), 2)]
    return parts[0]


def second_kernel(
    n_narrow, packed_ref, slots_ref, rhs_ref, parts_ref, held0_ref, held1_ref, held2_ref, first_ref, share_ref
):
    first = summed(parts_ref)
    first_ref[...] = first
    lines = lines_of(first)
    at = lax.broadcasted_iota(jnp.int32, lines.shape, 1)
    entry_at = lax.broadcasted_iota(jnp.int32, lines.shape, 0)
    lines = jnp.where(at % 8 == entry_at, lines, 0.0)
    there = moved_by(lines, slots_ref[...], ((1,), (1,)))
    size = there.shape[1] // 2
    chips = size // n_narrow
    halves = [there[:, :size], there[:, size:]]
    at = lax.broadcasted_iota(jnp.int32, halves[0].shape, 1)
    row, column = at // chips, at % chips
    near = []
    for dx in (-1, 0, 1):
        for dy in (-1, 0, 1):
            sides = []
            for core in range(2):
                step = (core + dy) // 2
                move = (-(dx * chips + step)) % size
                value = halves[(core + dy) % 2]
                value = pltpu.roll(value, move, 1) if move else value
                keep = (row + dx >= 0) & (row + dx < n_narrow) & (column + step >= 0) & (column + step < chips)
                sides.append(jnp.where(keep, value, 0.0))
            near.append(jnp.concatenate(sides, axis=1))
    near.append(jnp.zeros_like(there))
    near = jnp.concatenate(near, axis=0)
    image = jnp.concatenate(
        [jnp.sum(packed_ref[a * SLOT : (a + 1) * SLOT, :] * near, axis=0, keepdims=True) for a in range(8)], axis=0
    )
    vector = rhs_ref[...] - flat_of(moved_by(image, slots_ref[...], ((1,), (0,))))
    share = share_of(vector, (held0_ref, held1_ref, held2_ref))
    for place in range(share_ref.shape[0]):
        share_ref[place] = share


def last_kernel(ids_ref, z_ref, local_ref, first_ref, parts_ref, out_ref, sol_ref):
    solution = first_ref[...] + summed(parts_ref)
    sol_ref[...] = solution
    lines = lines_of(solution)
    at = lax.broadcasted_iota(jnp.int32, lines.shape, 1)
    row = lax.broadcasted_iota(jnp.int32, lines.shape, 0)
    weights = jnp.sum(jnp.where(at == ids_ref[4] * 8 + row, lines, 0.0), axis=1, keepdims=True)
    for x in range(z_ref.shape[2]):
        for i in range(3):
            acc = local_ref[i, x]
            for a in range(8):
                acc = acc + weights[a : a + 1, :] * z_ref[a, i, x].astype(F32)
            out_ref[i, x] = acc


def call(kernel, out_shape, in_specs, scratch=(), flops=0, moved=0, name=None):
    return pl.pallas_call(
        kernel,
        out_shape=[
            shape if isinstance(shape, jax.ShapeDtypeStruct) else jax.ShapeDtypeStruct(shape, F32) for shape in out_shape
        ],
        in_specs=in_specs,
        out_specs=[VMEM] * len(out_shape),
        scratch_shapes=list(scratch),
        compiler_params=pltpu.CompilerParams(vmem_limit_bytes=24 * 2**20),
        cost_estimate=pl.CostEstimate(flops=flops, bytes_accessed=moved, transcendentals=0),
        name=name,
    )


def body(
    deflation,
    residual,
    stiffness,
    mass,
    stencil,
    local_inverse,
    inverse_factor,
    margin_range,
    neighbor_blocks,
):
    vectors, _, cells_x, cells_y, depth = deflation.shape
    n_narrow, size_z = lax.axis_size("narrow"), lax.axis_size("z")
    count = lax.axis_size(WIDE) * n_narrow
    n_near = n_narrow * size_z
    size_y = lax.axis_size("y")

    rounded = residual.astype(jnp.bfloat16)
    couplings = stencil.transpose(1, 2, 0)
    ids = neighbor_blocks.reshape(-1)
    ranges = margin_range.reshape(-1)

    def swaps(axis):
        size = lax.axis_size(axis)
        even = [(k, k ^ 1) for k in range(size)]
        odd = [(k, ((k + 1) ^ 1) - 1) for k in range(1, size - 1)]
        return even, odd, lax.axis_index(axis) % 2 == 0

    def exchanged(sending_low, sending_high, axis):
        even, odd, is_even = swaps(axis)

        def chosen(first, second):
            return jnp.concatenate([jnp.where(is_even, x, y) for x, y in zip(first, second)], axis=0)

        one = lax.ppermute(chosen(sending_high, sending_low), axis, even)
        two = lax.ppermute(chosen(sending_low, sending_high), axis, odd)
        return one, two, is_even

    vector_fields = deflation.reshape(3 * vectors, cells_x, cells_y, depth)
    fields = (vector_fields, rounded)
    one, two, is_even = exchanged([f[:, 0] for f in fields], [f[:, cells_x - 1] for f in fields], "narrow")

    def matrix(rows):
        return jax.ShapeDtypeStruct((rows, 256), jnp.bfloat16)

    zf, zy, sy, table, own_matrix, x_matrix, y_matrix = call(
        before_kernel,
        [
            (vectors, 3, cells_x, cells_y, depth),
            (2, vectors, 3, 8, depth),
            (2, 8, depth),
            (8, 128),
            matrix(9 * cells_x * cells_y),
            matrix(144),
            matrix(288),
        ],
        [SMEM, SMEM] + [VMEM] * 3,
        [pltpu.VMEM((1, 8, 128), F32)],
        flops=20_000_000,
        moved=1_000_000,
        name="before",
    )(couplings, ids, deflation, rounded, stiffness)
    def joined(rows, partner):
        return jnp.concatenate([rows, lax.ppermute(rows, "z", [(k, partner(k) % size_z) for k in range(size_z)])], axis=0)

    rows_z = joined(inverse_factor, lambda k: k ^ 1)
    one, two, table = lax.optimization_barrier((one, two, table))
    rows_z = joined(rows_z, lambda k: k ^ 2)
    xlo, xhi = jnp.where(is_even, two, one), jnp.where(is_even, one, two)

    def side(y):
        middle = jnp.concatenate([f[:, :, y] for f in fields], axis=0)
        return [jnp.concatenate([xlo[:, y : y + 1], middle, xhi[:, y : y + 1]], axis=1)]

    one, two, is_even = exchanged(side(0), side(cells_y - 1), WIDE)
    ylo, yhi = jnp.where(is_even, two, one), jnp.where(is_even, one, two)

    (table,) = call(
        inner_kernel,
        [(8, 128)],
        [VMEM] * 8,
        [pltpu.VMEM((3 * vectors, 8, 128), F32)],
        flops=10_000_000,
        moved=1_000_000,
        name="inner",
    )(own_matrix, x_matrix, zf, stiffness, mass, xlo, xhi, table)
    far_z = lax.ppermute(rows_z, "z", [(k, (k + 2 if k // 2 % 2 else k - 2) % size_z) for k in range(size_z)])
    all_z = jnp.concatenate([rows_z, far_z], axis=0)
    table, payload = call(
        outer_kernel,
        [(8, 128), (n_near, 1, SLOT * vectors)],
        [VMEM] * 6,
        [pltpu.VMEM((6 * vectors, 8, 128), F32)],
        flops=10_000_000,
        moved=2_000_000,
        name="outer",
    )(y_matrix, table, zy, sy, ylo, yhi)
    got = lax.all_to_all(payload, ("narrow", "z"), 0, 0)
    local, blocks = call(
        local_kernel,
        [(3, cells_x, cells_y, depth), (vectors, vectors, 9)],
        [SMEM] + [VMEM] * 7,
        [pltpu.VMEM((3, cells_y + 2, 2, 8, depth // 2), F32)] * 2,
        flops=2_000_000,
        moved=3_000_000,
        name="local",
    )(ranges, local_inverse.transpose(0, 1, 3, 2, 4), rounded, xlo, xhi, ylo, yhi, table)
    got, local = lax.optimization_barrier((got, local))
    got = [got] + [lax.ppermute(got, "y", [(k, k ^ step) for k in range(size_y)]) for step in range(1, size_y)]
    got = jnp.stack(got)
    other = lax.ppermute(got, "core", [(0, 1), (1, 0)])
    held = [rows_z, far_z, lax.ppermute(all_z, "core", [(0, 1), (1, 0)])]
    group = ("narrow", "y")
    members = lax.axis_size(group)

    def spread(share):
        return lax.all_to_all(share, group, 0, 0)

    row = lax.axis_index("y").astype(jnp.int32).reshape(1)
    core = lax.axis_index("core").astype(jnp.int32).reshape(1)
    flat = (count * vectors // 128, 128)
    packed, slots, rhs, share = call(
        functools.partial(first_kernel, n_narrow, size_z),
        [
            (SLOT * vectors, count),
            jax.ShapeDtypeStruct((count, count * vectors), jnp.bfloat16),
            flat,
            (members,) + flat,
        ],
        [SMEM] * 2 + [VMEM] * 5,
        [pltpu.VMEM((count, SLOT * vectors), F32)],
        flops=2_000_000,
        moved=3_000_000,
        name="first",
    )(row, core, got, other, *held)
    first, share = call(
        functools.partial(second_kernel, n_narrow),
        [flat, (members,) + flat],
        [VMEM] * 7,
        flops=2_000_000,
        moved=3_000_000,
        name="second",
    )(packed, slots, rhs, spread(share), *held)
    preconditioned, solved = call(
        last_kernel,
        [(3, cells_x, cells_y, depth), flat],
        [SMEM] + [VMEM] * 4,
        flops=1_000_000,
        moved=1_000_000,
        name="last",
    )(ids, deflation, local, first, spread(share))
    coarse_solution = solved.reshape(-1)
    blocks = blocks.transpose(2, 0, 1)
    return preconditioned, blocks.reshape(1, 1, 9, vectors, vectors), coarse_solution


def solution(mesh):
    n_narrow, n_wide = mesh.devices.shape
    fine = jax.sharding.Mesh(mesh.devices.reshape(n_narrow, n_wide // 16, 8, 2), ("narrow",) + WIDE)
    placed = (
        P(None, None, "narrow", WIDE, None),
        P(None, "narrow", WIDE, None),
        P("narrow", WIDE, None),
        P("narrow", WIDE, None),
        P(),
        P(None, None, "narrow", WIDE, None),
        P(("narrow",) + WIDE, None),
        P("narrow", WIDE, None, None),
        P("narrow", WIDE, None),
    )
    return jax.shard_map(
        body,
        mesh=fine,
        in_specs=placed,
        out_specs=(P(None, "narrow", WIDE, None), P("narrow", WIDE, None, None, None), P()),
        check_vma=False,
    )
```
